128 devices in a mesh: dp: 64 (over z_hi, y, x, core), tensor: 2 (over z_lo).
Axes of the slice: x: 4, y: 4, z: 4 (z_hi: 2, z_lo: 2; z = z_hi * 2 + z_lo), core: 2. Of those that a mesh axis runs over, the one named last changes fastest.
Arguments:
- inputs: bfloat16 [128, 250, 768], P('dp'), may hold values from -6 to 6
- cotangent: float32 [128, 250, 768], P('dp'), may hold values from -6 to 6
- first_gain: bfloat16 [2, 768], replicated, may hold values from 0.25 to 1.75
- first_shift: bfloat16 [2, 768], replicated, may hold values from -1.75 to 1.75
- w_query: bfloat16 [2, 768, 768], P(None, None, 'tensor'), may hold values from -0.21875 to 0.21875
- b_query: bfloat16 [2, 768], P(None, 'tensor'), may hold values from -1.75 to 1.75
- w_key: bfloat16 [2, 768, 768], P(None, None, 'tensor'), may hold values from -0.21875 to 0.21875
- w_value: bfloat16 [2, 768, 768], P(None, None, 'tensor'), may hold values from -0.21875 to 0.21875
- b_value: bfloat16 [2, 768], P(None, 'tensor'), may hold values from -1.75 to 1.75
- w_out: bfloat16 [2, 768, 768], P(None, 'tensor'), may hold values from -0.875 to 0.875
- b_out: bfloat16 [2, 768], replicated, may hold values from -1.75 to 1.75
- second_gain: bfloat16 [2, 768], replicated, may hold values from 0.25 to 1.75
- second_shift: bfloat16 [2, 768], replicated, may hold values from -1.75 to 1.75
- w_up: bfloat16 [2, 768, 3072], P(None, None, 'tensor'), may hold values from -0.21875 to 0.21875
- b_up: bfloat16 [2, 3072], P(None, 'tensor'), may hold values from -1.75 to 1.75
- w_down: bfloat16 [2, 3072, 768], P(None, 'tensor'), may hold values from -0.109375 to 0.109375
- b_down: bfloat16 [2, 768], replicated, may hold values from -1.75 to 1.75
Outputs:
- activations: bfloat16 [128, 250, 768], P('dp')
- input_grad: float32 [128, 250, 768], P('dp')
- grad_first_gain: float32 [2, 768], replicated
- grad_first_shift: float32 [2, 768], replicated
- grad_w_query: float32 [2, 768, 768], P(None, None, 'tensor')
- grad_b_query: float32 [2, 768], P(None, 'tensor')
- grad_w_key: float32 [2, 768, 768], P(None, None, 'tensor')
- grad_w_value: float32 [2, 768, 768], P(None, None, 'tensor')
- grad_b_value: float32 [2, 768], P(None, 'tensor')
- grad_w_out: float32 [2, 768, 768], P(None, 'tensor')
- grad_b_out: float32 [2, 768], replicated
- grad_second_gain: float32 [2, 768], replicated
- grad_second_shift: float32 [2, 768], replicated
- grad_w_up: float32 [2, 768, 3072], P(None, None, 'tensor')
- grad_b_up: float32 [2, 3072], P(None, 'tensor')
- grad_w_down: float32 [2, 3072, 768], P(None, 'tensor')
- grad_b_down: float32 [2, 768], replicated
The draws below stay inside these ranges and needn't reach their ends.
All inputs are finite; a program needn't handle non-finite values.
Results may differ from the reference program's by a relative error of at most 0.015.
Values sent between devices are 32-bit elements; how exact they have to be, the bound alone decides.
A program may use at most 192 MiB of HBM per device.

```python
import jax
import jax.numpy as jnp
from jax import lax

D = 768
HEADS = 12
HEAD_DIM = 64
FF = 3072
FRAMES = 250
LAYERS = 2
CLIPS = 128


def level_of(key, dims, shards, smallest, largest):
    def one(axis_at, shards_of):
        draws = jax.random.uniform(jax.random.fold_in(jax.random.fold_in(key, 6), axis_at), (shards_of,), jnp.float32, smallest / len(shards), largest / len(shards))
        return jnp.repeat(jnp.exp(draws), dims[axis_at] // shards_of).reshape((-1,) + (1,) * (len(dims) - axis_at - 1))

    level = one(*shards[0])
    for cut in shards[1:]:
        level = level * one(*cut)
    return level


def scatter_about(key, shape, width, reach, shards=(), held_as=jnp.bfloat16):
    drawn = jax.random.normal(key, shape, jnp.float32) * width
    if len(shards) > 0:
        drawn = level_of(key, shape, shards, -0.22, 0.18) * drawn
    return jnp.clip(drawn, min=-reach, max=reach).astype(held_as)


def setup_inputs(seed: int = 0) -> dict:
    key_list = jax.random.split(jax.random.key(seed), 18)
    inputs = scatter_about(key_list[0], (CLIPS, FRAMES, D), 1.0, 6.0, ((0, 64),))
    cotangent = scatter_about(key_list[1], (CLIPS, FRAMES, D), 1.0, 6.0, ((0, 64),), jnp.float32)
    first_gain = jnp.clip(1.0 + 0.15 * jax.random.normal(key_list[2], (LAYERS, D), jnp.float32), 0.25, 1.75).astype(jnp.bfloat16)
    first_shift = scatter_about(key_list[3], (LAYERS, D), 0.3, 1.75)
    w_query = scatter_about(key_list[4], (LAYERS, D, D), D ** -0.5, 0.21875, ((2, 2),))
    b_query = scatter_about(key_list[5], (LAYERS, D), 0.3, 1.75, ((1, 2),))
    w_key = scatter_about(key_list[6], (LAYERS, D, D), D ** -0.5, 0.21875, ((2, 2),))
    w_value = scatter_about(key_list[7], (LAYERS, D, D), D ** -0.5, 0.21875, ((2, 2),))
    b_value = scatter_about(key_list[8], (LAYERS, D), 0.3, 1.75, ((1, 2),))
    w_out = scatter_about(key_list[9], (LAYERS, D, D), (D // 16) ** -0.5, 0.875, ((1, 2),))
    b_out = scatter_about(key_list[10], (LAYERS, D), 0.3, 1.75)
    second_gain = jnp.clip(1.0 + 0.15 * jax.random.normal(key_list[11], (LAYERS, D), jnp.float32), 0.25, 1.75).astype(jnp.bfloat16)
    second_shift = scatter_about(key_list[12], (LAYERS, D), 0.3, 1.75)
    w_up = scatter_about(key_list[13], (LAYERS, D, FF), D ** -0.5, 0.21875, ((2, 2),))
    b_up = scatter_about(key_list[14], (LAYERS, FF), 0.3, 1.75, ((1, 2),))
    w_down = scatter_about(key_list[15], (LAYERS, FF, D), FF ** -0.5, 0.109375, ((1, 2),))
    b_down = scatter_about(key_list[16], (LAYERS, D), 0.3, 1.75)
    return {"inputs": inputs, "cotangent": cotangent, "first_gain": first_gain, "first_shift": first_shift, "w_query": w_query, "b_query": b_query, "w_key": w_key, "w_value": w_value, "b_value": b_value, "w_out": w_out, "b_out": b_out, "second_gain": second_gain, "second_shift": second_shift, "w_up": w_up, "b_up": b_up, "w_down": w_down, "b_down": b_down}


@jax.custom_vjp
def low(v):
    return lax.optimization_barrier(v.astype(jnp.bfloat16)).astype(jnp.float32)

@jax.custom_vjp
def low_back(v):
    return v

def low_keep(v):
    return (low(v), None)

def low_pass(kept, grad):
    return (grad,)

def back_keep(v):
    return (v, None)

def back_low(kept, grad):
    return (low(grad),)
low.defvjp(low_keep, low_pass)
low_back.defvjp(back_keep, back_low)
EPSILON = 1e-05
HALF_ROOT = 0.7071067811865476
HIGHEST = lax.Precision.HIGHEST

def norm_rows(field_in, gain_row, shift_row):
    centre_val = field_in - lax.optimization_barrier(jnp.mean(field_in, axis=-1, keepdims=True))
    variance = lax.optimization_barrier(jnp.mean(centre_val * centre_val, axis=-1, keepdims=True))
    return centre_val * lax.rsqrt(variance + EPSILON) * gain_row + shift_row

def gelu_exact(before):
    return 0.5 * before * (1.0 + jax.scipy.special.erf(before * HALF_ROOT))

def attend(query_heads, key_heads, value_heads):
    scores = low_back(jnp.einsum('qhd,khd->hqk', query_heads, key_heads, precision=HIGHEST) * HEAD_DIM ** (-0.5))
    row_top = lax.optimization_barrier(jnp.max(scores, axis=-1, keepdims=True))
    weights = jnp.exp(scores - row_top)
    probs_all = weights / lax.optimization_barrier(jnp.sum(weights, axis=-1, keepdims=True))
    mixed_heads = jnp.einsum('hqk,khd->qhd', low(probs_all), value_heads, precision=HIGHEST)
    return low(low_back(mixed_heads)).reshape(FRAMES, D)

def forward(stream, first_gain, first_shift, w_query, b_query, w_key, w_value, b_value, w_out, b_out, second_gain, second_shift, w_up, b_up, w_down, b_down):
    attend_saved = jax.checkpoint(attend)
    for level in range(LAYERS):
        normed = low(norm_rows(stream, first_gain[level], first_shift[level]))
        query = low(low_back(jnp.dot(normed, w_query[level], precision=HIGHEST) + b_query[level]))
        keys_all = low(low_back(jnp.dot(normed, w_key[level], precision=HIGHEST)))
        values_all = low(low_back(jnp.dot(normed, w_value[level], precision=HIGHEST) + b_value[level]))
        shape_heads = (CLIPS, FRAMES, HEADS, HEAD_DIM)
        mixed = lax.map(lambda triple: attend_saved(triple[0], triple[1], triple[2]), (query.reshape(shape_heads), keys_all.reshape(shape_heads), values_all.reshape(shape_heads)))
        middle = stream + low_back(jnp.dot(mixed, w_out[level], precision=HIGHEST)) + b_out[level]
        normed_two = low(norm_rows(middle, second_gain[level], second_shift[level]))
        hidden = low_back(jnp.dot(normed_two, w_up[level], precision=HIGHEST) + b_up[level])
        activated = low(gelu_exact(hidden))
        stream = middle + low_back(jnp.dot(activated, w_down[level], precision=HIGHEST)) + b_down[level]
    return stream

def reference(inputs, cotangent, first_gain, first_shift, w_query, b_query, w_key, w_value, b_value, w_out, b_out, second_gain, second_shift, w_up, b_up, w_down, b_down):
    arrays = [inputs, first_gain, first_shift, w_query, b_query, w_key, w_value, b_value, w_out, b_out, second_gain, second_shift, w_up, b_up, w_down, b_down]
    arrays = [item.astype(jnp.float32) for item in arrays]
    result, pullback = jax.vjp(forward, *arrays)
    grads = pullback(cotangent.astype(jnp.float32))
    return (result.astype(jnp.bfloat16), grads[0], grads[1], grads[2], grads[3], grads[4], grads[5], grads[6], grads[7], grads[8], grads[9], grads[10], grads[11], grads[12], grads[13], grads[14], grads[15])
```

```python
import functools

import jax
import jax.numpy as jnp
from jax import lax
from jax.experimental import pallas as pl
from jax.experimental.pallas import tpu as pltpu
from jax.sharding import PartitionSpec as P

HEAD_DIM = 64
LAYERS = 2
D = 768
SUB = 768
SUBH = 192
GW = 256
KINDS = ("attn", "up", "down")
BLOCKS = tuple((level, kind) for level in range(LAYERS) for kind in KINDS)
ORDERS = (
    (("x", "y", "z"), ("y", "z", "x"), ("z", "x", "y")),
    (("y", "x", "z"), ("x", "z", "y"), ("z", "y", "x")),
)
STRIDES = ((192, 48, 24), (192, 96, 24), (384, 96, 24))
BACK_BLOCKS = tuple((level, kind) for level in (1, 0) for kind in ("down", "up", "attn"))
PAD = 256
UNIT = 192
SMALL_ROWS = 12 * LAYERS
VMEM_LIMIT = 63 * 1024 * 1024

EPSILON = 1e-05
HALF_ROOT = 0.7071067811865476
F32 = jnp.float32
BF16 = jnp.bfloat16
MESH = pl.DeviceIdType.MESH


class Place:
    def __init__(self):
        index = lax.axis_index("dp")
        self.t = lax.axis_index("tensor")
        self.core = lax.rem(index, 2)
        self.pos = {
            "x": lax.rem(lax.div(index, 2), 4),
            "y": lax.rem(lax.div(index, 8), 4),
            "z": lax.div(index, 32) * 2 + self.t,
        }

        self.steps = {(d, o): lax.rem(self.pos[d] + o, 4) for d in "xyz" for o in (1, 2, 3)}
        self.nears = {(d, o): self._device({**self.pos, d: at}, self.core) for (d, o), at in self.steps.items()}
        self.other_core = self._device(self.pos, 1 - self.core)
        self.other_half = self._device({**self.pos, "z": self.pos["z"] + 1 - 2 * self.t}, self.core)

    def _device(self, pos, core):
        z = pos["z"]
        index = ((lax.div(z, 2) * 4 + pos["y"]) * 4 + pos["x"]) * 2 + core
        return {"dp": index, "tensor": lax.rem(z, 2)}

    def at(self, dim, off):
        return self.steps[dim, off]

    def near(self, dim, off):
        return self.nears[dim, off]

    def sibling(self):
        return self.other_core

    def partner(self):
        return self.other_half


def greet(devices):
    barrier = pltpu.get_barrier_semaphore()
    for device in devices:
        pl.semaphore_signal(barrier, inc=1, device_id=device, device_id_type=MESH)
    pl.semaphore_wait(barrier, len(devices))


def remote(src, dst, send_sem, recv_sem, device):
    return pltpu.make_async_remote_copy(
        src_ref=src,
        dst_ref=dst,
        send_sem=send_sem,
        recv_sem=recv_sem,
        device_id=device,
        device_id_type=MESH,
    )


def push(src, dst, send_sem, recv_sem, device):
    remote(src, dst, send_sem, recv_sem, device).start()


def await_bytes(like, sem):
    pltpu.make_async_copy(like, like, sem).wait()


def rows_loop(total, step, body):
    if total <= step:
        body(pl.ds(0, total))
        return

    @pl.loop(0, total // step)
    def _(i):
        body(pl.ds(pl.multiple_of(i * step, step), step))


def m8(value):
    return pl.multiple_of(value, 8)


def halves(seg):
    first = (seg // 2 + 7) // 8 * 8
    return (0, first), (first, seg - first)


def ring_start(place, dim, view, rest, seg, send, fwd, rest_sem, source=None):
    mine = rest + place.pos[dim] * seg
    for off, order in ((1, (0, 1)), (3, (1, 0))):
        device = place.near(dim, off)
        for at, half in enumerate(order):
            sem = fwd.at[0 if off == 1 else 1] if at == 0 else rest_sem
            begin, rows = halves(seg)[half]
            piece = view(mine + begin, rows)
            push(source(begin, rows) if source else piece, piece, send, sem, device)


def ring_forward(place, dim, view, rest, seg, send, fwd, rest_sem):
    for which, off, half in ((0, 1, 0), (1, 3, 1)):
        begin, rows = halves(seg)[half]
        piece = view(rest + place.at(dim, 4 - off) * seg + begin, rows)
        await_bytes(piece, fwd.at[which])
        push(piece, piece, send, rest_sem, place.near(dim, off))


def ring_end(like, send, rest_sem):
    await_bytes(like(2), rest_sem)
    await_bytes(like(3), send)


def pair_start(place, view, rest, seg, stride, transit, send, fwd, source=None):
    mine = rest + lax.div(place.pos["z"], 2) * stride
    for which, off in ((0, 1), (1, 3)):
        begin, rows = halves(seg)[which]
        piece = source(begin, rows) if source else view(mine + begin, rows)
        push(piece, transit.at[which, pl.ds(0, rows)], send, fwd.at[which], place.near("z", off))


def pair_forward(place, view, rest, seg, stride, transit, send, fwd, rest_sem):
    for which, off in ((0, 1), (1, 3)):
        begin, rows = halves(seg)[which]
        row = rest + lax.div(place.at("z", 4 - off), 2) * stride + begin
        piece = transit.at[which, pl.ds(0, rows)]
        await_bytes(piece, fwd.at[which])
        push(piece, view(row, rows), send, rest_sem, place.near("z", off))


def pair_end(like, send, rest_sem):
    await_bytes(like(1), rest_sem)
    await_bytes(like(2), send)


class Plan:
    LINK = 88e3
    CORES = 300e3
    MEMORY = 1500e3
    DELAY = 2.0
    LOCAL = 1.6
    PUSH = 0.04
    WAIT = 0.02
    SLOWER = 1.0

    def __init__(self):
        self.steps = []
        self.events = {}
        self.queues = {}
        self.now = 4.0
        self.trail = []

    def add(self, name, run, cost=0.0, after=(), needs=(), sends=(), rank=0.0, kind=0):
        cost = cost * self.SLOWER if kind == 1 else cost
        self.steps.append((name, run, cost, tuple(after), tuple(needs), tuple(sends), rank, kind))
        return name

    def send(self, event, link, size):
        if link == MEMORY:
            there = self.now + self.LOCAL + size / self.MEMORY
        else:
            taken = size / self.CORES if link == CORES else 2 * size / self.LINK
            begin = max(self.now + 0.3, self.queues.get(link, 0.0))
            self.queues[link] = begin + taken
            there = begin + taken + self.DELAY
        self.events[event] = max(self.events.get(event, 0.0), there)

    def order(self):
        left = list(self.steps)
        done = set()
        runs = []
        while left:
            best, best_key = None, None
            for at, (name, run, cost, after, needs, sends, rank, kind) in enumerate(left):
                if not all(other in done for other in after):
                    continue
                ready = max([self.events[event] for event in needs], default=0.0)
                late = ready > self.now
                key = (late, ready if late else 0.0, kind, rank, at)
                if best is None or key < best_key:
                    best, best_key = at, key
            name, run, cost, after, needs, sends, rank, kind = left.pop(best)
            self.now = max([self.now] + [self.events[event] for event in needs])
            for event, link, size in sends:
                self.now += self.PUSH
                self.send(event, link, size)
            self.now += cost + self.WAIT * len(needs)
            done.add(name)
            self.trail.append((name, round(self.now, 1)))
            runs.append(run)
        return runs


PACK, SHARE, WIDE, OPEN, FORWARD, FETCH, READY, GRAD, START, MIDDLE, END, FINISH, SMALLS, BEGIN, PASS, CLOSE = range(16)
LEAD, REST, SUM, STAGED, FIRST, LAST, ALL, ACROSS = range(20, 28)
MEMORY, CORES = range(2)
BOTH_WAYS = ((1, 0), (3, 1))


class Gather:
    RINGS = (("x", "y"), ("y", "x"))

    def __init__(self, refs, place, layers):
        self.__dict__.update(refs)
        self.place = place
        self.layers = layers
        self.shares = (
            place.pos["y"] * UNIT + place.pos["x"] * 48,
            place.pos["x"] * UNIT + place.pos["y"] * 48,
        )

    def view(self, b, g):
        def view(row, rows):
            return self.landed.at[b, g, lax.div(row, UNIT), pl.ds(m8(lax.rem(row, UNIT)), rows)]

        return view

    def share(self, b, g):
        n = 2 * b + g
        return self.pool.at[36 + n // 4, pl.ds(48 * (n % 4), 48)]

    def cross_share(self, b):
        own = self.layers.weight(BLOCKS[b][0], BLOCKS[b][1], 0)
        for g in range(2):
            row = pl.multiple_of(self.shares[g], 16)
            small = self.share(b, g)
            small[...] = own[pl.ds(row, 48), g * GW : (g + 1) * GW].astype(F32)
            for n, off in ((0, 1), (1, 3)):
                push(
                    small.at[pl.ds(24 * n, 24)],
                    self.view(b, g)(self.shares[g] + 24 * n, 24),
                    self.z_send.at[b, g],
                    self.z_recv.at[b, g],
                    self.place.near("z", off),
                )

    def cross_wide(self, b):
        own = self.layers.weight(BLOCKS[b][0], BLOCKS[b][1], 0)
        for r in range(4):
            for top in range(0, UNIT, 64):
                self.pool[4 * b + r, top : top + 64, :] = own[r * UNIT + top : r * UNIT + top + 64, 2 * GW :].astype(F32)
        for n, off in ((0, 1), (1, 3)):
            push(
                self.pool.at[pl.ds(4 * b + 2 * n, 2)],
                self.landed.at[b, 2, pl.ds(2 * n, 2)],
                self.z_send.at[b, 2],
                self.z_recv.at[b, 2],
                self.place.near("z", off),
            )

    def ring(self, b, g, at, part):
        dim = self.RINGS[g][at]
        seg = (48, UNIT)[at]
        rest = self.place.pos[self.RINGS[g][1]] * UNIT if at == 0 else 0
        view = self.view(b, g)
        send, fwd, rest_sem = self.ring_send.at[b, g, at], self.ring_fwd.at[b, g, at], self.ring_rest.at[b, g, at]
        if part == 0:
            ring_start(self.place, dim, view, rest, seg, send, fwd, rest_sem)
        elif part == 1:
            ring_forward(self.place, dim, view, rest, seg, send, fwd, rest_sem)
        elif at == 0:
            ring_end(lambda k: self.landed.at[b, g, 0, pl.ds(0, 48 * k)], send, rest_sem)
        else:
            ring_end(lambda k: self.landed.at[b, g, pl.ds(0, k)], send, rest_sem)

    def load(self, b, g):
        return pltpu.make_async_copy(self.landed.at[b, g], self.pool.at[pl.ds(24 + 4 * g, 4)], self.low_sem.at[g])

    def fetch(self, b, g):
        if g < 2:
            self.ring(b, g, 1, 2)
            self.load(b, g).start()
            await_bytes(self.share(b, g), self.z_send.at[b, g])
        else:
            await_bytes(self.landed.at[b, 2], self.z_recv.at[b, 2])
            self.load(b, g).start()
            await_bytes(self.landed.at[b, 2], self.z_send.at[b, 2])

    def convert(self, b, g):
        self.load(b, g).wait()

        @pl.loop(0, 4)
        def _(r):
            for top in range(0, UNIT, 64):
                rows = pl.ds(pl.multiple_of(r * UNIT + top, 64), 64)
                self.w[b, 1, rows, g * GW : (g + 1) * GW] = self.pool[24 + 4 * g + r, top : top + 64, :].astype(BF16)

    def ring_open(self, b, g, at):
        if at == 0:
            await_bytes(self.share(b, g), self.z_recv.at[b, g])
        else:
            self.ring(b, g, 0, 2)
        self.ring(b, g, at, 0)

    def schedule(self, plan):
        row = 4 * GW

        def z_both(event, size):
            return [(event, ("z", way), size) for way in (1, 3)]

        before = None
        for kind, b in [(kind, b) for kind in (SHARE, WIDE) for b in range(6)]:
            after = [(PACK, b // 3)] + ([before] if before else [])
            if kind == SHARE:
                sends = [send for g in range(2) for send in z_both((SHARE, b, g), 24 * row)]
                before = plan.add((SHARE, b), functools.partial(self.cross_share, b), 0.2, after, (), sends, 2.5)
            else:
                sends = z_both((WIDE, b), 384 * row)
                before = plan.add((WIDE, b), functools.partial(self.cross_wide, b), 0.5, after, (), sends, 2.5)
        for b in range(len(BLOCKS)):
            for g in range(2):
                previous = (SHARE, b)
                for at in range(2):
                    dim = self.RINGS[g][at]
                    half = (48, UNIT)[at] * row // 2
                    needs = [(SHARE, b, g)] if at == 0 else [(REST, b, g, 0)]
                    sends = []
                    for off, which in BOTH_WAYS:
                        sends += [((LEAD, b, g, at, which), (dim, off), half), ((REST, b, g, at), (dim, off), half)]
                    after = [previous]
                    if at and b:
                        after.append((FORWARD, b - 1, g, 1))
                    elif b > 1:
                        after.append((OPEN, b - 2, g, 1))
                    opened = plan.add((OPEN, b, g, at), functools.partial(self.ring_open, b, g, at), 0.0, after, needs, sends, b)
                    needs = [(LEAD, b, g, at, which) for which in range(2)]
                    sends = [((REST, b, g, at), (dim, off), half) for off, which in BOTH_WAYS]
                    run = functools.partial(self.ring, b, g, at, 1)
                    previous = plan.add((FORWARD, b, g, at), run, 0.0, [opened], needs, sends, b)
            for g in range(3):
                after = [(FORWARD, b, g, 1) if g < 2 else (WIDE, b)] + ([(READY, b - 1, g)] if b else [])
                needs = [(REST, b, g, 1)] if g < 2 else [(WIDE, b)]
                sends = [((FETCH, b, g), MEMORY, D * row)]
                fetched = plan.add((FETCH, b, g), functools.partial(self.fetch, b, g), 0.0, after, needs, sends, b)
                plan.add((READY, b, g), functools.partial(self.convert, b, g), 0.45, [fetched], [(FETCH, b, g)], (), b)


ROW_UP = 6
ROW_QKV = 8
SUBHEADS = SUBH // HEAD_DIM
QKV = 640
INV_ROOT_TAU = 0.3989422804014327


def dot(first_op, second_op):
    return jnp.dot(first_op, second_op, preferred_element_type=F32)


def dot_rows(first_op, second_op):
    return lax.dot_general(first_op, second_op, (((1,), (1,)), ((), ())), preferred_element_type=F32)


def row_sum(array):
    return jnp.sum(array, axis=0, keepdims=True)


class Layers:
    def __init__(self, refs, place, frames):
        self.__dict__.update(refs)
        self.place = place
        self.frames = frames
        self.sums = 0
        self.pending = {}
        self.waiting = {}
        self.stage_at = 0


    def weight(self, level, kind, s):
        b = 3 * level + KINDS.index(kind)
        if (b, s) in self.waiting:
            self.waiting.pop((b, s)).wait()
        return self.w.at[b, s]

    def attn_loads(self, level, w_query, w_key, w_value, w_out):
        low = pl.ds(0, 2 * SUBH)
        if level == 0:
            spots = [self.gt.at[1, 0, :, low], self.gt.at[1, 1, :, low], self.gt.at[0, 0, :, low]]
        else:
            spots = [self.gt.at[0, 1, :, low], self.h2t.at[0, :, low], self.h2t.at[1, :, low]]
        last = self.du.at[level, pl.ds(0, SUBH)]
        rows = pl.ds(pl.multiple_of(self.place.core * SUBH, 16), SUBH)
        sources = [w_query.at[level], w_key.at[level], w_value.at[level], w_out.at[level, rows]]
        return [pltpu.make_async_copy(a, b, self.attn_sem.at[level, n]) for n, (a, b) in enumerate(zip(sources, spots + [last]))]

    def attn_pack(self, level, copies):
        b = 3 * level
        for copy in copies:
            copy.wait()
        spots = [copy.dst_ref for copy in copies]
        for c in range(2):

            @pl.when(self.place.core == c)
            def _():
                def body(rows):
                    parts = [spot[rows, c * SUBH : (c + 1) * SUBH] for spot in spots[:3]]
                    self.w[b, 0, rows, : 3 * SUBH] = jnp.concatenate(parts, axis=1)

                rows_loop(D, 64, body)

        self.w[b, 0, :, 3 * SUBH :] = spots[3][...].T


    def sum_copy(self, n, c):
        rows = pl.ds(c * PAD, PAD)
        return remote(
            self.part.at[rows], self.land.at[n % 2, rows], self.sum_send.at[n, c], self.sum_recv.at[n, c], self.place.sibling()
        )

    def sum_start(self, n, c):
        self.sum_copy(n, c).start()

    def summed(self, n, c):
        self.sum_copy(n, c).wait()
        return lambda rows: self.part[rows, :] + self.land[n % 2, rows, :]

    def tile_loop(self, c, body, step=64):
        @pl.loop(0, PAD // step)
        def _(i):
            at = pl.multiple_of(i * step, step)
            body(pl.ds(pl.multiple_of(c * PAD + at, step), step), pl.ds(at, step))

    def vector(self, level, row):
        if row in (ROW_UP + 1, ROW_QKV + 1):
            at = 8 * level + (0 if row == ROW_UP + 1 else 1)
            return self.bias_other[at : at + 1, :]
        return self.vec[level, row : row + 1, :]

    @staticmethod
    def centred(x):
        c = x - jnp.mean(x, axis=-1, keepdims=True)
        return c, lax.rsqrt(jnp.mean(c * c, axis=-1, keepdims=True) + EPSILON)


    def f_attend(self, level, c, n_in):
        gain, shift = self.vector(level, 0), self.vector(level, 1)
        if level == 0:
            before = None
        else:
            before, b_down = self.summed(n_in, c), self.vector(level - 1, 5)

        def body(rows, at):
            if before is None:
                x = self.x[0, rows, :]
            else:
                x = self.mid[level - 1, rows, :] + before(rows) + b_down
                self.x[level, rows, :] = x
            centre, root = self.centred(x)
            self.hb[rows, :] = (centre * root * gain + shift).astype(BF16)

        self.tile_loop(c, body)
        rows = slice(c * PAD, (c + 1) * PAD)
        self.h1t[level, :, rows] = self.hb[rows, :].T

    def f_project(self, level, c, s):
        rows = slice(c * PAD, (c + 1) * PAD)
        h = self.hb[rows, :]
        wa = self.weight(level, "attn", s)
        bias = self.vector(level, ROW_QKV + s)
        for lo, hi in ((0, 256), (256, 512), (512, QKV)):
            value = (dot(h, wa[:, lo:hi]) + bias[:, lo:hi]).astype(BF16)
            if lo == 0:
                query = lax.broadcasted_iota(jnp.int32, (PAD, 256), 1) < SUBH
                value = jnp.where(query, value * HEAD_DIM**-0.5, value)
            self.qkv[level, s, rows, lo:hi] = value

    def f_mix(self, level, c, s):
        rows = slice(c * PAD, (c + 1) * PAD)
        block = self.qkv[level, s, rows, :]
        heads = [self.heads(block, head) for head in range(SUBHEADS)]
        scores = [self.masked(dot_rows(k, q)) for q, k, v in heads]
        tops = [jnp.max(score, axis=0, keepdims=True) for score in scores]
        exps = [jnp.exp(score - top) for score, top in zip(scores, tops)]
        totals = [row_sum(value) for value in exps]
        mixed = [dot(v.T, value.astype(BF16)) for (q, k, v), value in zip(heads, exps)]
        for head, (top, total) in enumerate(zip(tops, totals)):
            at = SUBHEADS * s + head
            self.lse[level, c, at : at + 1, :] = top + jnp.log(total)
        mixed = [jnp.zeros((HEAD_DIM, PAD), F32)] + [value * (1.0 / total) for value, total in zip(mixed, totals)]
        self.a[level, s, rows, :] = jnp.concatenate(mixed, axis=0).T.astype(BF16)

    def masked(self, scores):
        edge = self.frames // 8 * 8
        last = lax.broadcasted_iota(jnp.int32, (PAD - edge, PAD), 0) < self.frames - edge
        return jnp.concatenate([scores[:edge], jnp.where(last, scores[edge:], -1e30)], axis=0)

    def f_out(self, level, c, n_out):
        rows = slice(c * PAD, (c + 1) * PAD)
        for lo in range(0, D, GW):
            out = [dot_rows(self.a[level, s, rows, :], self.weight(level, "attn", s)[lo : lo + GW, 512:D]) for s in range(2)]
            self.part[rows, lo : lo + GW] = out[0] + out[1]
        self.sum_start(n_out, c)

    @staticmethod
    def heads(block, head):
        lo = head * HEAD_DIM
        return tuple(block[:, n * SUBH + lo : n * SUBH + lo + HEAD_DIM] for n in range(3))

    def f_up(self, level, c, n_in):
        gain, shift, b_out = self.vector(level, 2), self.vector(level, 3), self.vector(level, 4)
        branch = self.summed(n_in, c)

        def body(rows, at):
            x = self.x[level, rows, :] + branch(rows) + b_out
            self.mid[level, rows, :] = x
            centre, root = self.centred(x)
            self.hb[rows, :] = (centre * root * gain + shift).astype(BF16)

        self.tile_loop(c, body)
        rows = slice(c * PAD, (c + 1) * PAD)
        self.h2t[level, :, rows] = self.hb[rows, :].T

    def f_hidden(self, level, c, s):
        rows = slice(c * PAD, (c + 1) * PAD)
        h = self.hb[rows, :]
        wu = self.weight(level, "up", s)
        bias = self.vector(level, ROW_UP + s)
        for lo in range(0, SUB, GW):
            self.u[:, lo : lo + GW] = dot(h, wu[:, lo : lo + GW]) + bias[:, lo : lo + GW]

        def gelu(rows, at):
            u = self.u[at, :]
            half = 0.5 + 0.5 * lax.erf(u * HALF_ROOT)
            self.du[s, rows, :] = (u * half).astype(BF16)
            self.gp[level, s, rows, :] = (half + u * (jnp.exp(u * u * -0.5) * INV_ROOT_TAU)).astype(BF16)

        self.tile_loop(c, gelu, 32)
        self.gt[level, s, :, rows] = self.du[s, rows, :].T

    def f_down(self, level, c, n_out):
        rows = slice(c * PAD, (c + 1) * PAD)
        for lo in range(0, D, GW):
            out = [dot(self.du[s, rows, :], self.weight(level, "down", s)[:, lo : lo + GW]) for s in range(2)]
            self.part[rows, lo : lo + GW] = out[0] + out[1]
        self.sum_start(n_out, c)

    def f_end(self, n_in):
        for c in range(2):
            total = self.summed(n_in, c)

            @pl.when(self.place.core == c)
            def _():
                def body(rows, at):
                    self.u[at, :] = self.mid[LAYERS - 1, rows, :] + total(rows) + self.vector(LAYERS - 1, 5)

                self.tile_loop(c, body)


    def add_row(self, level, row, value):
        at = 12 * level + row
        self.small[at : at + 1, :] = self.small[at : at + 1, :] + value

    def norm_back(self, level, c, total, x_ref, gain_row, grad_row, after):
        gain = self.vector(level, gain_row)

        def body(rows, at):
            dh = total(rows)
            centre, root = self.centred(x_ref[level, rows, :])
            n = centre * root
            self.add_row(level, grad_row, row_sum(dh * n))
            self.add_row(level, grad_row + 1, row_sum(dh))
            dn = dh * gain
            shift = jnp.mean(dn, axis=-1, keepdims=True)
            slope = jnp.mean(dn * n, axis=-1, keepdims=True)
            dx = self.dx[rows, :] + root * (dn - shift - n * slope)
            self.dx[rows, :] = dx
            after(rows, at, dx)

        self.tile_loop(c, body)

    def b_low(self, level, c):
        def body(rows, at):
            dx = self.dx[rows, :]
            self.add_row(level, 5, row_sum(dx))
            self.dm[rows, :] = dx.astype(BF16)

        self.tile_loop(c, body)

    def b_hidden(self, level, c, s):
        rows = slice(c * PAD, (c + 1) * PAD)
        dm = self.dm[rows, :]
        wd = self.weight(level, "down", s)
        sums = []
        for lo in range(0, SUB, GW):
            dg = dot_rows(dm, wd[lo : lo + GW, :])
            du = (dg * self.gp[level, s, rows, lo : lo + GW].astype(F32)).astype(BF16)
            self.du[s, rows, lo : lo + GW] = du
            sums.append(row_sum(du.astype(F32)))
        self.add_row(level, ROW_UP + s, jnp.concatenate(sums, axis=1))

    def b_up(self, level, c, n_out):
        rows = slice(c * PAD, (c + 1) * PAD)
        for lo in range(0, D, GW):
            out = [dot_rows(self.du[s, rows, :], self.weight(level, "up", s)[lo : lo + GW, :]) for s in range(2)]
            self.part[rows, lo : lo + GW] = out[0] + out[1]
        self.sum_start(n_out, c)

    def stage_copy(self, slot, b, s, g):
        return pltpu.make_async_copy(self.staged.at[slot], self.grads.at[b, s, g], self.stage_sem.at[slot])

    def settle(self, b):
        for slot, key in list(self.pending.items()):
            if key[0] == b:
                self.stage_copy(slot, *key).wait()
                self.pending.pop(slot)

    def grad(self, key, s, left, right, extra=None):
        b = BACK_BLOCKS.index(key)
        for g in range(3):
            slot = self.stage_at % 4
            self.stage_at += 1
            if slot in self.pending:
                self.stage_copy(slot, *self.pending.pop(slot)).wait()
            value = dot(left[...], right[:, g * GW : (g + 1) * GW])
            if extra is not None and g == 2:
                value = value + dot(extra[0][...], extra[1][...])
            self.staged[slot] = value.reshape(4, UNIT, GW)
            self.stage_copy(slot, b, s, g).start()
            self.pending[slot] = (b, s, g)

    def b_grad_down(self, level, s):
        self.grad((level, "down"), s, self.gt.at[level, s], self.dm)

    def b_grad_up(self, level, s):
        self.grad((level, "up"), s, self.h2t.at[level], self.du.at[s])

    def b_grad_attn(self, level, s):
        self.grad((level, "attn"), s, self.h1t.at[level], self.du.at[s], (self.dbt, self.a.at[level, s]))

    def b_attend(self, level, c, n_in):
        total = self.summed(n_in, c)

        def after(rows, at, dx):
            self.add_row(level, 4, row_sum(dx))
            self.hb[rows, :] = dx.astype(BF16)

        self.norm_back(level, c, total, self.mid, 2, 2, after)
        rows = slice(c * PAD, (c + 1) * PAD)
        self.dbt[:, rows] = self.hb[rows, :].T

    def b_mix(self, level, c, s):
        rows = slice(c * PAD, (c + 1) * PAD)
        da = dot(self.hb[rows, :], self.weight(level, "attn", s)[:, 512:D]).astype(BF16)
        block = self.qkv[level, s, rows, :]
        heads = [self.heads(block, head) for head in range(SUBHEADS)]
        da_heads = [da[:, HEAD_DIM * (head + 1) : HEAD_DIM * (head + 2)] for head in range(SUBHEADS)]
        scores = [self.masked(dot_rows(k, q)) for q, k, v in heads]
        d_probs = [dot_rows(v, da_head) for (q, k, v), da_head in zip(heads, da_heads)]
        at = SUBHEADS * s
        probs = [jnp.exp(score - self.lse[level, c, at + head : at + head + 1, :]) for head, score in enumerate(scores)]
        dv = [dot(value.astype(BF16), da_head).astype(BF16) for value, da_head in zip(probs, da_heads)]
        d_scores = [(p * (dp - row_sum(p * dp))).astype(BF16) for p, dp in zip(probs, d_probs)]
        dk = [dot(value, q).astype(BF16) for (q, k, v), value in zip(heads, d_scores)]
        dq = [dot(k.T, value) * HEAD_DIM**-0.5 for (q, k, v), value in zip(heads, d_scores)]
        d_query = jnp.concatenate(dq, axis=0).T.astype(BF16)
        zeros = jnp.zeros((PAD, D - 3 * SUBH), BF16)
        block = jnp.concatenate([d_query] + dk + dv + [zeros], axis=1)
        self.du[s, rows, :] = block
        self.add_row(level, ROW_QKV + s, row_sum(block.astype(F32)))

    def b_in(self, level, c, n_out):
        rows = slice(c * PAD, (c + 1) * PAD)
        for lo in range(0, D, GW):
            out = [
                dot_rows(self.du[s, rows, :QKV], self.weight(level, "attn", s)[lo : lo + GW, :QKV]) for s in range(2)
            ]
            self.part[rows, lo : lo + GW] = out[0] + out[1]
        self.sum_start(n_out, c)

    def b_first(self, level, c, n_in):
        total = self.summed(n_in, c)

        def after(rows, at, dx):
            if level > 0:
                self.add_row(level - 1, 5, row_sum(dx))
                self.dm[rows, :] = dx.astype(BF16)

        self.norm_back(level, c, total, self.x, 0, 0, after)

    def schedule(self, plan, pack, take_cot, leave_act, finish):
        last = LAYERS - 1
        clip_bytes = 4 * PAD * D
        chain = []

        def add(run, cost, *args, name=None, after=(), needs=(), sends=()):
            name = name or (-1, len(chain))
            chain.append(plan.add(name, functools.partial(run, *args), cost, list(after) + chain[-1:], needs, sends, 0.0, 1))

        def ready(level, kind):
            b = 3 * level + KINDS.index(kind)
            return [(READY, b, g) for g in range(3)]

        def summing(n, c):
            return [((SUM, n, c), CORES, clip_bytes)]

        def staging(level, kind):
            return [((STAGED, BACK_BLOCKS.index((level, kind))), MEMORY, 4 * D * D)]

        def grad(run, cost, level, kind):
            for s in range(2):
                add(run, cost, level, s, name=(GRAD, level, kind, s), sends=staging(level, kind))

        add(pack, 1.0, 0, name=(PACK, 0))
        add(pack, 1.0, 1, name=(PACK, 1))
        n = 0
        for level in range(LAYERS):
            for c in range(2):
                add(self.f_attend, 0.7, level, c, n - 1, needs=[(SUM, n - 1, c)] if level else ())
                add(self.f_project, 0.4, level, c, 0)
                add(self.f_mix, 1.6, level, c, 0)
            if level == 0:
                add(take_cot, 0.1)
                for c in range(2):
                    add(self.b_low, 0.3, last, c)
            for c in range(2):
                add(self.f_project, 0.4, level, c, 1, after=ready(level, "attn"))
                add(self.f_mix, 1.6, level, c, 1)
                add(self.f_out, 0.5, level, c, n, sends=summing(n, c))
            for c in range(2):
                add(self.f_up, 0.8, level, c, n, needs=[(SUM, n, c)])
                add(self.f_hidden, 1.4, level, c, 0)
            for c in range(2):
                add(self.f_hidden, 1.4, level, c, 1, after=ready(level, "up"))
                if level < last:
                    add(self.f_down, 0.7, level, c, n + 1, after=ready(level, "down"), sends=summing(n + 1, c))
            n += 2
        grad(self.b_grad_down, 1.1, last, "down")
        for c in range(2):
            add(self.f_down, 0.7, last, c, n - 1, after=ready(last, "down"), sends=summing(n - 1, c))
        for level in reversed(range(LAYERS)):
            for c in range(2):
                if level < last:
                    add(self.b_first, 1.0, level + 1, c, n - 1, needs=[(SUM, n - 1, c)])
                for s in range(2):
                    add(self.b_hidden, 0.7, level, c, s)
                if level == last and c == 0:
                    add(self.f_end, 0.5, n - 1, needs=[(SUM, n - 1, 0), (SUM, n - 1, 1)])
                    add(leave_act, 0.1, sends=[((ACROSS, 0), ("z", 1), clip_bytes)])
                add(self.b_up, 0.7, level, c, n, sends=summing(n, c))
            if level < last:
                grad(self.b_grad_down, 1.1, level, "down")
            grad(self.b_grad_up, 1.1, level, "up")
            for c in range(2):
                add(self.b_attend, 1.2, level, c, n, needs=[(SUM, n, c)])
                for s in range(2):
                    add(self.b_mix, 2.4, level, c, s)
                add(self.b_in, 0.8, level, c, n + 1, sends=summing(n + 1, c))
            grad(self.b_grad_attn, 1.4, level, "attn")
            n += 2
        for c in range(2):
            add(self.b_first, 1.0, 0, c, n - 1, needs=[(SUM, n - 1, c)])
        add(finish, 0.5, name=(FINISH, 0), sends=[((ACROSS, 1), ("z", 1), clip_bytes)])


COMPUTE_SCRATCH = dict(
    w=((len(BLOCKS), 2, D, D), BF16),
    x=((LAYERS, 2 * PAD, D), F32),
    mid=((LAYERS, 2 * PAD, D), F32),
    dx=((2 * PAD, D), F32),
    part=((2 * PAD, D), F32),
    land=((2, 2 * PAD, D), F32),
    h1t=((LAYERS, D, 2 * PAD), BF16),
    h2t=((LAYERS, D, 2 * PAD), BF16),
    qkv=((LAYERS, 2, 2 * PAD, QKV), BF16),
    a=((LAYERS, 2, 2 * PAD, 256), BF16),
    lse=((LAYERS, 2, 8, PAD), F32),
    gt=((LAYERS, 2, SUB, 2 * PAD), BF16),
    gp=((LAYERS, 2, 2 * PAD, SUB), BF16),
    hb=((2 * PAD, D), BF16),
    u=((PAD, SUB), F32),
    dm=((2 * PAD, D), BF16),
    du=((2, 2 * PAD, SUB), BF16),
    dbt=((D, 2 * PAD), BF16),
    staged=((4, 4, UNIT, GW), F32),
    small=((SMALL_ROWS, D), F32),
    small_all=((3, 4, SMALL_ROWS, D), F32),
    sum_three=((6, 3, 24, GW), F32),
    bias_other=((8 * LAYERS, D), F32),
    bias_own=((8 * LAYERS, D), F32),
    vec=((LAYERS, 16, D), F32),
    pool=((48, UNIT, GW), F32),
    first_two=((3, 2, 3, 48, GW), F32),
    last_two=((3, 4, 3, 48, GW), F32),
    sum_two=((3, 2, 3, 48, GW), F32),
    heard_three=((3, 6, 6, 24, 128), F32),
)
SUMS = 4 * LAYERS


class Reduce:
    BUNDLES = ((0, 1), (1, 1), (2, 1), (3, 2), (5, 1))

    def __init__(self, refs, place, layers):
        self.__dict__.update(refs)
        self.place = place
        self.layers = layers


    def span(self, n, phase):
        return (n, 1) if phase == 0 else self.BUNDLES[n]

    def holder(self, b):
        return next(n for n, (first, count) in enumerate(self.BUNDLES) if first <= b - 3 < first + count)

    def slot(self, n):
        return self.BUNDLES[n][0] % 3

    def order(self, n, phase):
        return ORDERS[self.span(n, phase)[0] // 3]

    def set_of(self, z):
        return lax.rem(lax.rem(z, 2) + self.place.t, 2)

    def unit(self, n, g, phase, chunk, part):
        first, count = self.span(n, phase)
        low, high = lax.rem(chunk, 2), lax.div(chunk, 2)
        if phase == 0:
            which, row = (part, chunk) if g < 2 else (self.set_of(chunk), 2 * high + part)
            return self.grads.at[n, which, g, row]
        if phase == 1:
            if g == 0:
                which, row = part, chunk * 48
            elif g == 1:
                which, row = self.set_of(chunk), high * 96 + part * 48
            else:
                which, row = high, low * 96 + part * 48
            return self.pool.at[pl.ds(30 + (2 * g + which) * 3 + self.slot(n), count), pl.ds(m8(row), 48)]
        which, row = (self.set_of(chunk), high) if g == 0 else (high, low)
        return self.sum_two.at[g, which, pl.ds(self.slot(n), count), pl.ds(m8(row * 24), 24), pl.ds(128 * part, 128)]

    def result(self, n, g, phase, part):
        first, count = self.span(n, phase)
        if phase == 0:
            return self.pool.at[30 + (2 * g + part) * 3 + n % 3]
        if phase == 1:
            return self.sum_two.at[g, part, pl.ds(self.slot(n), count)]
        return self.sum_three.at[pl.ds(first, count), g, :, pl.ds(128 * part, 128)]

    def heard(self, n, g, phase, slots):
        first, count = self.span(n, phase)
        if phase == 0:
            return self.heard_one.at[g, slots, n]
        return (self.heard_two, self.heard_three)[phase - 1].at[g, slots, pl.ds(first, count)]

    def pool_part(self, base, slots):
        if isinstance(slots, int):
            return self.pool.at[base + slots]
        return self.pool.at[pl.ds(base + slots.start, slots.size)]

    def first_box(self, n, g, phase, parts):
        count = self.span(n, phase)[1]
        if phase == 0:
            return self.pool_part(6 + 6 * (n % 2) + 2 * g, parts)
        if phase == 1:
            return self.first_two.at[g, parts, pl.ds(0, count)]
        return self.heard(n, g, phase, parts)

    def last_box(self, n, g, phase, slots):
        count = self.span(n, phase)[1]
        if phase == 0:
            return self.pool_part(18 + 4 * g, slots)
        if phase == 1:
            return self.last_two.at[g, slots, pl.ds(0, count)]
        if isinstance(slots, int):
            return self.heard(n, g, phase, slots + 2)
        return self.heard(n, g, phase, pl.ds(2, 4))

    def blocks(self, n, phase, *refs):
        if phase == 0:
            return [refs]
        return [tuple(ref.at[block] for ref in refs) for block in range(self.span(n, phase)[1])]

    def rs_start(self, n, g, phase):
        place = self.place
        if phase == 0:
            self.layers.settle(n)
        dim = self.order(n, phase)[g][phase]
        send, first, rest = self.rs_send.at[n, g, phase], self.rs_first.at[n, g, phase], self.rs_rest.at[n, g, phase]
        far = place.at(dim, 2)
        right, left = place.near(dim, 1), place.near(dim, 3)

        def out(chunk, part, slot, sem, device):
            unit = self.unit(n, g, phase, chunk, part)
            push(unit, self.heard(n, g, phase, slot), send, sem, device)

        out(far, 0, 0, first, right)
        out(far, 1, 1, first, left)
        out(place.at(dim, 1), 1, 3, rest, right)
        out(place.at(dim, 3), 0, 4, rest, left)

    def side_load(self, n, g, part):
        source = self.unit(n, g, 0, self.place.at(self.order(n, 0)[g][0], 1 if part == 0 else 3), part)
        return pltpu.make_async_copy(source, self.pool.at[2 * g + part], self.side_sem.at[g])

    def first_load(self, n, g, phase):
        both = pl.ds(0, 2)
        source, target = self.heard(n, g, phase, both), self.first_box(n, g, phase, both)
        return pltpu.make_async_copy(source, target, self.middle_sem.at[phase, g])

    def rs_middle_load(self, n, g, phase):
        if phase == 0:
            for part in range(2):
                self.side_load(n, g, part).start()
        await_bytes(self.heard(n, g, phase, pl.ds(0, 2)), self.rs_first.at[n, g, phase])
        self.first_load(n, g, phase).start()

    def rs_middle(self, n, g, phase):
        place = self.place
        dim = self.order(n, phase)[g][phase]
        if phase < 2:
            self.first_load(n, g, phase).wait()
        else:
            await_bytes(self.heard(n, g, phase, pl.ds(0, 2)), self.rs_first.at[n, g, phase])
        if phase == 0:
            await_bytes(self.pool.at[pl.ds(2 * g, 2)], self.side_sem.at[g])
        for part, off, slot in ((0, 1, 2), (1, 3, 5)):
            mine = self.first_box(n, g, phase, part)
            side = self.pool.at[2 * g + part] if phase == 0 else self.unit(n, g, phase, place.at(dim, off), part)
            for total, add in self.blocks(n, phase, mine, side):

                def body(rows):
                    total[rows, :] = total[rows, :] + add[rows, :]

                rows_loop(total.shape[0], 96, body)
            push(mine, self.heard(n, g, phase, slot), self.rs_send.at[n, g, phase], self.rs_rest.at[n, g, phase], place.near(dim, off))

    def last_load(self, n, g, phase):
        source, target = self.heard(n, g, phase, pl.ds(2, 4)), self.last_box(n, g, phase, pl.ds(0, 4))
        return pltpu.make_async_copy(source, target, self.end_sem.at[phase, g])

    def rs_end_load(self, n, g, phase):
        if phase == 0:
            for part in range(2):
                source = self.unit(n, g, 0, self.place.pos[self.order(n, 0)[g][0]], part)
                pltpu.make_async_copy(source, self.result(n, g, 0, part), self.mine_sem.at[g]).start()
        await_bytes(self.heard(n, g, phase, pl.ds(2, 4)), self.rs_rest.at[n, g, phase])
        self.last_load(n, g, phase).start()

    def rs_end(self, n, g, phase):
        if phase < 2:
            self.last_load(n, g, phase).wait()
        else:
            await_bytes(self.heard(n, g, phase, pl.ds(2, 4)), self.rs_rest.at[n, g, phase])
        if phase == 0:
            await_bytes(self.pool.at[pl.ds(30, 2)], self.mine_sem.at[g])
        for part in range(2):
            results = self.result(n, g, phase, part)
            own = results if phase == 0 else self.unit(n, g, phase, self.place.pos[self.order(n, phase)[g][phase]], part)
            lows, highs = self.last_box(n, g, phase, part), self.last_box(n, g, phase, 2 + part)
            for out, start, low, high in self.blocks(n, phase, results, own, lows, highs):

                def body(rows):
                    out[rows, :] = start[rows, :] + (low[rows, :] + high[rows, :])

                rows_loop(out.shape[0], 96, body)
        await_bytes(self.heard(n, g, phase, pl.ds(0, 6)), self.rs_send.at[n, g, phase])
        if phase == 1:
            self.rs_start(n, g, 2)

    def schedule(self, plan):
        units = [4 * UNIT * GW, 4 * 48 * GW, 4 * 24 * 128]

        def add(name, run, *args, cost=0.0, after=(), needs=(), sends=()):
            after = [step for step in after if step[1] >= 0]
            rank = 0.001 * (name[1] if name[3] == 0 else self.BUNDLES[name[1]][0])
            return plan.add(name, functools.partial(run, *name[1:3], *args), cost, after, needs, sends, rank)

        def opening(n, g, phase):
            dim, size = self.order(n, phase)[g][phase], units[phase] * self.span(n, phase)[1]
            sends = [((FIRST, n, g, phase), (dim, off), size) for off, _ in BOTH_WAYS]
            return sends + [((LAST, n, g, phase), (dim, off), size) for off, _ in BOTH_WAYS]

        def rest(n, g, phase, after):
            dim, size = self.order(n, phase)[g][phase], units[phase] * self.span(n, phase)[1]
            heard = (FIRST, n, g, phase)
            if phase < 2:
                pool = [(READY, b, part) for b in range(len(BLOCKS)) for part in range(3)]
                hold = pool + [(MIDDLE, n - 1, g, 0), (END, n - 2, g, 0)] if phase == 0 else [(END, n - 1, g, 1)]
                loads = [((MIDDLE, n, g, phase), MEMORY, size)] * (3 if phase == 0 else 1)
                after = [add((OPEN, n, g, phase, MIDDLE), self.rs_middle_load, phase, after=after + hold, needs=[heard], sends=loads)]
                heard = (MIDDLE, n, g, phase)
            sends = [((LAST, n, g, phase), (dim, off), size) for off, _ in BOTH_WAYS]
            after = [add((MIDDLE, n, g, phase), self.rs_middle, phase, cost=2e-6 * size, after=after, needs=[heard], sends=sends)]
            heard = (LAST, n, g, phase)
            if phase < 2:
                hold = [(END, n - 1, g, phase)] + ([(END, self.holder(n), g, 1)] if phase == 0 and n >= 3 else [])
                loads = [((END, n, g, phase), MEMORY, 2 * size)] * (3 if phase == 0 else 1)
                after = [add((OPEN, n, g, phase, END), self.rs_end_load, phase, after=after + hold, needs=[heard], sends=loads)]
                heard = (END, n, g, phase)
            if phase == 1:
                first, count = self.BUNDLES[n]
                after = after + [(END, self.holder(b), g, 2) for b in range(max(first, 3), first + count)]
            sends = opening(n, g, 2) if phase == 1 else ()
            return [add((END, n, g, phase), self.rs_end, phase, cost=3e-6 * size, after=after, needs=[heard], sends=sends)]

        for g in range(3):
            for b, (level, kind) in enumerate(BACK_BLOCKS):
                grads = [(GRAD, level, kind, s) for s in range(2)]
                rest(b, g, 0, [add((START, b, g, 0), self.rs_start, 0, after=grads, needs=[(STAGED, b)], sends=opening(b, g, 0))])
            for n, (first, count) in enumerate(self.BUNDLES):
                ready = [(END, b, g, 0) for b in range(first, first + count)]
                after = rest(n, g, 1, [add((START, n, g, 1), self.rs_start, 1, after=ready, sends=opening(n, g, 1))])
                rest(n, g, 2, after)


class Spread:
    EARLY_Z = (0, 1, 2, 3, 4)

    def __init__(self, refs, place):
        self.__dict__.update(refs)
        self.place = place

    def view(self, b, g):
        level, kind = BACK_BLOCKS[b]
        core = self.place.core
        columns = pl.ds(g * GW, GW)
        if kind == "up":
            return lambda row, rows: self.out_up.at[level, pl.ds(m8(row), rows), pl.ds(pl.multiple_of(core * SUB + g * GW, 128), GW)]
        if kind == "down":
            return lambda row, rows: self.out_down.at[level, pl.ds(m8(core * SUB + row), rows), columns]
        return lambda row, rows: self.out_attn.at[level, core, g, pl.ds(m8(row), rows)]

    def own_copy(self, b, g):
        phase, seg, _ = self.route(b, g)[0]
        row = self.spots(b, g, 0)[0] + self.where(ORDERS[b // 3][g][phase]) * seg
        return pltpu.make_async_copy(self.sum_three.at[b, g], self.view(b, g)(row, seg), self.own_sem.at[b, g])

    def where(self, dim):
        return lax.div(self.place.pos["z"], 2) if dim == "z" else self.place.pos[dim]

    @staticmethod
    def route(b, g):
        strides = STRIDES[g]
        if g == 2 and b in Spread.EARLY_Z:
            return ((2, strides[2], 1), (0, strides[1], 1), (1, strides[1], 2))
        return tuple((phase, strides[phase], 1) for phase in (2, 1, 0))

    def spots(self, b, g, step):
        route = self.route(b, g)
        done = {phase for phase, _, _ in route[: step + 1]}
        row = 0
        for n in range(3):
            if n not in done:
                row = row + self.where(ORDERS[b // 3][g][n]) * STRIDES[g][n]
        return [row + part * STRIDES[g][0] for part in range(route[step][2])]

    def ag(self, b, g, step, part):
        phase, seg, count = self.route(b, g)[step]
        dim = ORDERS[b // 3][g][phase]
        view = self.view(b, g)
        like = lambda k: view(0, k * seg)
        transit = (self.transit_0, self.transit_1, self.transit_2)[g].at[b] if dim == "z" else None
        for n, rest in enumerate(self.spots(b, g, step)):
            send, fwd, rest_sem = (array.at[b, g, step, n] for array in (self.ag_send, self.ag_fwd, self.ag_rest))
            if part == 0:
                source = None
                if step == 0:
                    self.own_copy(b, g).start()
                    source = lambda row, rows: self.sum_three.at[b, g, pl.ds(row, rows)]
                if dim == "z":
                    pair_start(self.place, view, rest, seg, STRIDES[g][phase], transit, send, fwd, source)
                else:
                    ring_start(self.place, dim, view, rest, seg, send, fwd, rest_sem, source)
            elif part == 1:
                if dim == "z":
                    pair_forward(self.place, view, rest, seg, STRIDES[g][phase], transit, send, fwd, rest_sem)
                else:
                    ring_forward(self.place, dim, view, rest, seg, send, fwd, rest_sem)
            elif dim == "z":
                pair_end(like, send, rest_sem)
            else:
                ring_end(like, send, rest_sem)

    def start(self, b, g):
        self.ag(b, g, 0, 0)

    def last(self, b, g):
        phase, seg, count = self.route(b, g)[2]
        return ORDERS[b // 3][g][phase], seg, self.spots(b, g, 2)

    def forward(self, b, g, step):
        self.ag(b, g, step, 1)
        dim, seg, rests = self.last(b, g)
        if step == 2 and dim != "z":
            for rest in rests:
                self.across(b, g, rest + self.place.at(dim, 3) * seg, halves(seg)[0])
                self.across(b, g, rest + self.place.at(dim, 1) * seg, halves(seg)[1])

    def end(self, b, g, step):
        self.ag(b, g, step, 2)
        if step == 0:
            self.own_copy(b, g).wait()
        dim, seg, rests = self.last(b, g)
        if step < 2:
            self.ag(b, g, step + 1, 0)
            if step == 1:
                for rest in rests:
                    self.across(b, g, rest + self.where(dim) * seg, (0, seg))
            return
        for rest in rests:
            if dim == "z":
                self.across(b, g, rest + (1 - self.where(dim)) * seg, (0, seg))
            else:
                self.across(b, g, rest + self.place.at(dim, 3) * seg, halves(seg)[1])
                self.across(b, g, rest + self.place.at(dim, 1) * seg, halves(seg)[0])
                self.across(b, g, rest + self.place.at(dim, 2) * seg, (0, seg))

    def across(self, b, g, row, span):
        piece = self.view(b, g)(row + span[0], span[1])
        push(piece, piece, self.d2d_send.at[b, g], self.d2d_recv.at[b, g], self.place.sibling())

    def across_end(self, b, g):
        whole = self.view(b, g)(0, D)
        remote(whole, whole, self.d2d_send.at[b, g], self.d2d_recv.at[b, g], self.place.sibling()).wait()


    def small_start(self, n):
        dim = "xyz"[n]
        mine = self.small_all.at[n, self.place.pos[dim]]
        mine[...] = self.small[...]
        for off in (1, 2, 3):
            push(mine, mine, self.misc_send.at[3 + n], self.misc_recv.at[3 + n], self.place.near(dim, off))

    def small_end(self, n):
        await_bytes(self.small_all.at[n, pl.ds(0, 3)], self.misc_recv.at[3 + n])
        await_bytes(self.small_all.at[n, pl.ds(0, 3)], self.misc_send.at[3 + n])
        self.small[...] = (self.small_all[n, 0] + self.small_all[n, 1]) + (self.small_all[n, 2] + self.small_all[n, 3])

    def small_copy(self):
        return remote(
            self.small, self.small_both.at[self.place.core], self.misc_send.at[6], self.misc_recv.at[6], self.place.sibling()
        )

    def small_share(self):
        self.small_both[self.place.core] = self.small[...]
        self.small_copy().start()

    def schedule(self, plan):
        before = [(FINISH, 0)]
        for n in range(3):
            sends = [((SMALLS, n), ("xyz"[n], off), 8 * SMALL_ROWS * D) for off in (1, 3)]
            before = [plan.add((SMALLS, n, 0), functools.partial(self.small_start, n), 0.1, before, (), sends, -1.0)]
            before = [plan.add((SMALLS, n, 1), functools.partial(self.small_end, n), 0.1, before, [(SMALLS, n)], (), -1.0)]
        plan.add((SMALLS, 3, 0), self.small_share, 0.1, before)
        for n, (first, count) in enumerate(Reduce.BUNDLES):
            for b, g in ((b, g) for b in range(first, first + count) for g in range(3)):

                def add(name, run, *args, after=(), needs=(), sends=()):
                    return plan.add(name, functools.partial(run, b, g, *args), 0.0, after, needs, sends, 0.001 * b, 2 if b else 0)

                route = self.route(b, g)

                def gathering(step):
                    phase, seg, count = route[step]
                    dim, half = ORDERS[b // 3][g][phase], seg * 512
                    sends = []
                    for off, which in BOTH_WAYS:
                        sends += [((LEAD, b, g, step, which), (dim, off), half)] * count
                        if dim != "z":
                            sends += [((ALL, b, g, step), (dim, off), half)] * count
                    return sends

                after = [add((BEGIN, b, g), self.start, after=[(END, n, g, 2)], sends=gathering(0))]
                for step, (phase, seg, count) in enumerate(route):
                    dim, half = ORDERS[b // 3][g][phase], seg * 512
                    lead = [(LEAD, b, g, step, which) for which in range(2)]
                    sends = [((ALL, b, g, step), (dim, off), half) for off, _ in BOTH_WAYS] * count
                    if step == 2 and dim != "z":
                        sends += [((ACROSS, b, g), CORES, half)] * 2 * count
                    after = [add((PASS, b, g, step), self.forward, step, after=after, needs=lead, sends=sends)]
                    if step < 2:
                        sends = gathering(step + 1)
                        if step == 1:
                            sends += [((ACROSS, b, g), CORES, route[2][1] * 1024)] * route[2][2]
                        if step == 1 and b and ORDERS[b // 3][g][route[2][0]] != "z":
                            after = after + [(PASS, b - 1, g, 2)]
                    else:
                        sends = [((ACROSS, b, g), CORES, half * 2)] * (1 if dim == "z" else 2 * count)
                    after = [add((CLOSE, b, g, step), self.end, step, after=after, needs=[(ALL, b, g, step)], sends=sends)]
                add((ACROSS, b, g), self.across_end, after=after + [(FINISH, 0)], needs=[(ACROSS, b, g)])


DMA_ARRAYS = dict(
    sum_send=(SUMS, 2),
    sum_recv=(SUMS, 2),
    w_sem=(len(BLOCKS), 2),
    x_sem=(4,),
    attn_sem=(LAYERS, 4),
    stage_sem=(4,),
    out_sem=(2,),
    z_send=(len(BLOCKS), 3),
    z_recv=(len(BLOCKS), 3),
    ring_send=(len(BLOCKS), 2, 2),
    ring_fwd=(len(BLOCKS), 2, 2, 2),
    ring_rest=(len(BLOCKS), 2, 2),
    low_sem=(3,),
    side_sem=(3,),
    middle_sem=(2, 3),
    end_sem=(2, 3),
    mine_sem=(3,),
    rs_send=(len(BLOCKS), 3, 3),
    rs_first=(len(BLOCKS), 3, 3),
    rs_rest=(len(BLOCKS), 3, 3),
    misc_send=(7,),
    misc_recv=(7,),
    ag_send=(len(BLOCKS), 3, 3, 2),
    ag_fwd=(len(BLOCKS), 3, 3, 2, 2),
    ag_rest=(len(BLOCKS), 3, 3, 2),
    own_sem=(len(BLOCKS), 3),
    d2d_send=(len(BLOCKS), 3),
    d2d_recv=(len(BLOCKS), 3),
)
HBM_ARRAYS = dict(
    out_up=(LAYERS, D, 2 * SUB),
    out_down=(LAYERS, 2 * SUB, D),
    out_attn=(LAYERS, 2, 3, D, GW),
    pair_own=(2, PAD, D),
    pair_far=(2, PAD, D),
    grads=(len(BLOCKS), 2, 3, 4, UNIT, GW),
    landed=(len(BLOCKS), 3, 4, UNIT, GW),
    heard_one=(3, 6, len(BLOCKS), UNIT, GW),
    heard_two=(3, 6, len(BLOCKS), 48, GW),
    transit_0=(len(BLOCKS), 2, 16, GW),
    transit_1=(len(BLOCKS), 2, 48, GW),
    transit_2=(len(BLOCKS), 2, 192, GW),
)


def step_kernel(frames, x_in, cot_in, w_query, w_key, w_value, w_out, up_own, down_own, *rest):
    place = Place()
    core, t = place.core, place.t
    vectors, rest = rest[:9], rest[9:]
    names = ["small_both"] + list(HBM_ARRAYS) + list(COMPUTE_SCRATCH) + list(DMA_ARRAYS)
    refs = dict(zip(names, rest))
    vec, bias_own = refs["vec"], refs["bias_own"]
    run = Layers(refs, place, frames)
    gather = Gather(refs, place, run)
    reduce = Reduce(refs, place, run)
    misc_send, misc_recv = refs["misc_send"], refs["misc_recv"]
    columns = pl.ds(pl.multiple_of(core * SUB, 128), SUB)
    rows = pl.ds(pl.multiple_of(core * SUB, 16), SUB)
    mine = pl.ds(pl.multiple_of(core * PAD, PAD), PAD)
    attn_loads = [run.attn_loads(level, w_query, w_key, w_value, w_out) for level in range(LAYERS)]
    for b, (level, kind) in enumerate(BLOCKS):
        if kind == "attn":
            for copy in attn_loads[level]:
                copy.start()
            continue
        source = up_own.at[level, :, columns] if kind == "up" else down_own.at[level, rows, :]
        run.waiting[b, 0] = pltpu.make_async_copy(source, run.w.at[b, 0], run.w_sem.at[b, 0])
        run.waiting[b, 0].start()
    clips = (x_in.at[t], cot_in.at[t])
    local = [
        pltpu.make_async_copy(clips[0], run.x.at[0, mine], run.x_sem.at[0]),
        pltpu.make_async_copy(clips[1], run.dx.at[mine], run.x_sem.at[1]),
    ]
    for copy in local:
        copy.start()

    for n in range(ROW_UP):
        vec[:, n, :] = vectors[n][...].astype(F32)
    query_bias, value_bias, up_bias = (vector[...].astype(F32) for vector in vectors[ROW_UP:])
    for c in range(2):

        @pl.when(core == c)
        def _():
            span = slice(c * SUBH, (c + 1) * SUBH)
            nothing = jnp.zeros((LAYERS, SUBH), F32)
            rows_up = up_bias[:, c * SUB : (c + 1) * SUB]
            rows_qkv = jnp.concatenate([query_bias[:, span], nothing, value_bias[:, span], nothing], axis=1)
            for level in range(LAYERS):
                line = slice(level, level + 1)
                for row, value in ((0, rows_up), (1, rows_qkv)):
                    bias_own[8 * level + row : 8 * level + row + 1, :] = value[line]
                vec[level, ROW_UP : ROW_UP + 1, :] = rows_up[line]
                vec[level, ROW_QKV : ROW_QKV + 1, :] = rows_qkv[line]

    greet([place.near(d, o) for d in "xyz" for o in (1, 2, 3)] + [place.sibling()])
    given = [
        remote(clips[0], run.x.at[0, mine], misc_send.at[0], misc_recv.at[0], place.sibling()),
        remote(bias_own, run.bias_other, misc_send.at[1], misc_recv.at[1], place.partner()),
        remote(clips[1], run.dx.at[mine], misc_send.at[2], misc_recv.at[2], place.sibling()),
    ]
    for copy in given:
        copy.start()

    run.small[...] = jnp.zeros_like(run.small)
    outs = [
        pltpu.make_async_copy(run.u, refs["pair_own"].at[0], run.out_sem.at[0]),
        pltpu.make_async_copy(run.dx.at[mine], refs["pair_own"].at[1], run.out_sem.at[1]),
    ]
    far = [
        remote(run.u, refs["pair_far"].at[0], misc_send.at[0], misc_recv.at[0], place.partner()),
        remote(run.dx.at[mine], refs["pair_far"].at[1], misc_send.at[1], misc_recv.at[1], place.partner()),
    ]

    def pack(level):
        run.attn_pack(level, attn_loads[level])
        if level == LAYERS - 1:
            local[0].wait()
            given[0].wait()
            given[1].wait()

    def take_cot():
        local[1].wait()
        given[2].wait()

    def leave_act():
        outs[0].start()
        far[0].start()

    def leave():
        outs[1].start()
        far[1].start()
        for level in range(LAYERS):
            for base in (ROW_UP, ROW_QKV):
                at = 12 * level + base
                pair = run.small[at : at + 2, :]
                swapped = jnp.concatenate([pair[1:2], pair[0:1]], axis=0)
                run.small[at : at + 2, :] = jnp.where(t == 0, pair, swapped)

    plan = Plan()
    run.schedule(plan, pack, take_cot, leave_act, leave)
    gather.schedule(plan)
    reduce.schedule(plan)
    spread = Spread(refs, place)
    spread.schedule(plan)
    for write in plan.order():
        write()
    spread.small_copy().wait()
    for copy in outs + far:
        copy.wait()


def step(frames, x, cot, weights, vectors):
    anywhere = pl.BlockSpec(memory_space=pl.ANY)
    vmem = pl.BlockSpec(memory_space=pltpu.VMEM)
    return pl.pallas_call(
        functools.partial(step_kernel, frames),
        out_shape=tuple(
            jax.ShapeDtypeStruct(shape, F32) for shape in ((2, SMALL_ROWS, D), *HBM_ARRAYS.values())
        ),
        in_specs=[anywhere] * 8 + [vmem] * len(vectors),
        out_specs=(vmem,) + (anywhere,) * len(HBM_ARRAYS),
        scratch_shapes=[pltpu.VMEM(*spec) for spec in COMPUTE_SCRATCH.values()]
        + [pltpu.SemaphoreType.DMA(shape) for shape in DMA_ARRAYS.values()],
        compiler_params=pltpu.CompilerParams(collective_id=0, has_side_effects=True, vmem_limit_bytes=VMEM_LIMIT),
        name="step",
    )(x, cot, *weights, *vectors)


def tidy_kernel(frames, small, own, far, attn_in, act, grad_in, *rest):
    rows_out, outs, (attn, packed, packed_out, load_sem, store_sem) = rest[:9], rest[9:13], rest[13:]
    t = lax.axis_index("tensor")
    loads = [pltpu.make_async_copy(attn_in.at[level], attn.at[level], load_sem.at[level]) for level in range(LAYERS)]
    for copy in loads:
        copy.start()
    stores = []
    for level in range(LAYERS):
        loads[level].wait()

        def body(rows):
            for n in range(3):
                parts = []
                for s in range(2):
                    block = [attn[level, s, g, rows, :] for g in range(3)]
                    pieces = (
                        [block[0][:, :SUBH]],
                        [block[0][:, SUBH:], block[1][:, :128]],
                        [block[1][:, 128:], block[2][:, :64]],
                    )
                    parts += pieces[n]
                packed[level, n, rows, :] = jnp.concatenate(parts, axis=1)

        rows_loop(D, 64, body)
        for s in range(2):
            packed_out[level, s * SUBH : (s + 1) * SUBH, :] = attn[level, s, 2][:, 64:].T
        for n in range(4):
            source = packed.at[level, n] if n < 3 else packed_out.at[level]
            stores.append(pltpu.make_async_copy(source, outs[n].at[level], store_sem.at[level, n]))
            stores[-1].start()
    for n, out in ((0, act), (1, grad_in)):
        first = jnp.where(t == 0, own[n], far[n])[:frames]
        second = jnp.where(t == 0, far[n], own[n])[:frames]
        out[...] = jnp.stack([first, second], axis=1).astype(out.dtype)
    step = SMALL_ROWS // LAYERS
    for level in range(LAYERS):
        line = slice(level, level + 1)
        for n in range(ROW_UP):
            at = step * level + n
            rows_out[n][line, :] = small[0, at : at + 1, :]
        up = step * level + ROW_UP + t
        qkv = step * level + ROW_QKV + t
        for s in range(2):
            row = small[s, pl.ds(qkv, 1), :]
            rows_out[6][line, s * SUBH : (s + 1) * SUBH] = row[:, :SUBH]
            rows_out[7][line, s * SUBH : (s + 1) * SUBH] = row[:, 2 * SUBH : 3 * SUBH]
            rows_out[8][line, s * SUB : (s + 1) * SUB] = small[s, pl.ds(up, 1), :]
    for copy in stores:
        copy.wait()


def tidy(frames, small, pair_own, pair_far, attn):
    vmem = pl.BlockSpec(memory_space=pltpu.VMEM)
    anywhere = pl.BlockSpec(memory_space=pl.ANY)
    shapes = [((frames, 2, D), BF16), ((frames, 2, D), F32)]
    shapes += [((LAYERS, D), F32)] * 6 + [((LAYERS, 2 * SUBH), F32)] * 2 + [((LAYERS, 2 * SUB), F32)]
    wide = [((LAYERS, D, 2 * SUBH), F32)] * 3 + [((LAYERS, 2 * SUBH, D), F32)]
    act, grad_in, *rest = pl.pallas_call(
        functools.partial(tidy_kernel, frames),
        out_shape=[jax.ShapeDtypeStruct(*spec) for spec in shapes + wide],
        in_specs=[vmem] * 3 + [anywhere],
        out_specs=[vmem] * len(shapes) + [anywhere] * len(wide),
        scratch_shapes=[
            pltpu.VMEM((LAYERS, 2, 3, D, GW), F32),
            pltpu.VMEM((LAYERS, 3, D, 2 * SUBH), F32),
            pltpu.VMEM((LAYERS, 2 * SUBH, D), F32),
            pltpu.SemaphoreType.DMA((LAYERS,)),
            pltpu.SemaphoreType.DMA((LAYERS, 4)),
        ],
        compiler_params=pltpu.CompilerParams(vmem_limit_bytes=VMEM_LIMIT),
        name="tidy",
    )(small, pair_own, pair_far, attn)
    return [act.transpose(1, 0, 2), grad_in.transpose(1, 0, 2)] + rest


def local(
    inputs, cotangent, first_gain, first_shift, w_query, b_query, w_key, w_value, b_value, w_out, b_out,
    second_gain, second_shift, w_up, b_up, w_down, b_down,
):
    frames = inputs.shape[1]

    def padded(array):
        return jnp.pad(array.astype(F32), ((0, 0), (0, PAD - frames), (0, 0)))

    small, g_up, g_down, attn, pair_own, pair_far, *unused = step(
        frames, padded(inputs), padded(cotangent), (w_query, w_key, w_value, w_out, w_up, w_down),
        (first_gain, first_shift, second_gain, second_shift, b_out, b_down, b_query, b_value, b_up),
    )
    (
        act, grad_in, g_first_gain, g_first_shift, g_second_gain, g_second_shift, g_b_out, g_b_down, g_b_query, g_b_value, g_b_up,
        g_query, g_key, g_value, g_out,
    ) = tidy(frames, small, pair_own, pair_far, attn)
    return (
        act, grad_in, g_first_gain, g_first_shift, g_query, g_b_query, g_key, g_value, g_b_value, g_out, g_b_out,
        g_second_gain, g_second_shift, g_up, g_b_up, g_down, g_b_down,
    )


def solution(mesh):
    rows3 = P("dp", None, None)
    cols3 = P(None, None, "tensor")
    mid3 = P(None, "tensor", None)
    cols2 = P(None, "tensor")
    layout = (P(), P(), cols3, cols2, cols3, cols3, cols2, mid3, P(), P(), P(), cols3, cols2, mid3, P())
    return jax.shard_map(
        local,
        mesh=mesh,
        in_specs=(rows3, rows3) + layout,
        out_specs=(rows3, rows3) + layout,
        check_vma=False,
    )
```

```python
import functools

import jax
import jax.numpy as jnp
from jax import lax
from jax.experimental import pallas as pl
from jax.experimental.pallas import tpu as pltpu
from jax.sharding import PartitionSpec as P

HEAD_DIM = 64
LAYERS = 2
D = 768
SUB = 768
SUBH = 192
GW = 256
KINDS = ("attn", "up", "down")
BLOCKS = tuple((level, kind) for level in range(LAYERS) for kind in KINDS)
ORDERS = (
    (("x", "y", "z"), ("y", "z", "x"), ("z", "x", "y")),
    (("y", "x", "z"), ("x", "z", "y"), ("z", "y", "x")),
)
STRIDES = ((192, 48, 24), (192, 96, 24), (384, 96, 24))
BACK_BLOCKS = tuple((level, kind) for level in (1, 0) for kind in ("down", "up", "attn"))
PAD = 256
UNIT = 192
SMALL_ROWS = 12 * LAYERS
VMEM_LIMIT = 63 * 1024 * 1024

EPSILON = 1e-05
HALF_ROOT = 0.7071067811865476
F32 = jnp.float32
BF16 = jnp.bfloat16
MESH = pl.DeviceIdType.MESH


class Place:
    def __init__(self):
        index = lax.axis_index("dp")
        self.t = lax.axis_index("tensor")
        self.core = lax.rem(index, 2)
        self.pos = {
            "x": lax.rem(lax.div(index, 2), 4),
            "y": lax.rem(lax.div(index, 8), 4),
            "z": lax.div(index, 32) * 2 + self.t,
        }

        self.steps = {(d, o): lax.rem(self.pos[d] + o, 4) for d in "xyz" for o in (1, 2, 3)}
        self.nears = {(d, o): self._device({**self.pos, d: at}, self.core) for (d, o), at in self.steps.items()}
        self.other_core = self._device(self.pos, 1 - self.core)
        self.other_half = self._device({**self.pos, "z": self.pos["z"] + 1 - 2 * self.t}, self.core)

    def _device(self, pos, core):
        z = pos["z"]
        index = ((lax.div(z, 2) * 4 + pos["y"]) * 4 + pos["x"]) * 2 + core
        return {"dp": index, "tensor": lax.rem(z, 2)}

    def at(self, dim, off):
        return self.steps[dim, off]

    def near(self, dim, off):
        return self.nears[dim, off]

    def sibling(self):
        return self.other_core

    def partner(self):
        return self.other_half


def greet(devices):
    barrier = pltpu.get_barrier_semaphore()
    for device in devices:
        pl.semaphore_signal(barrier, inc=1, device_id=device, device_id_type=MESH)
    pl.semaphore_wait(barrier, len(devices))


def remote(src, dst, send_sem, recv_sem, device):
    return pltpu.make_async_remote_copy(
        src_ref=src,
        dst_ref=dst,
        send_sem=send_sem,
        recv_sem=recv_sem,
        device_id=device,
        device_id_type=MESH,
    )


def push(src, dst, send_sem, recv_sem, device):
    remote(src, dst, send_sem, recv_sem, device).start()


def await_bytes(like, sem):
    pltpu.make_async_copy(like, like, sem).wait()


def rows_loop(total, step, body):
    if total <= step:
        body(pl.ds(0, total))
        return

    @pl.loop(0, total // step)
    def _(i):
        body(pl.ds(pl.multiple_of(i * step, step), step))


def m8(value):
    return pl.multiple_of(value, 8)


def halves(seg):
    first = (seg // 2 + 7) // 8 * 8
    return (0, first), (first, seg - first)


def ring_start(place, dim, view, rest, seg, send, fwd, rest_sem, source=None):
    mine = rest + place.pos[dim] * seg
    for off, order in ((1, (0, 1)), (3, (1, 0))):
        device = place.near(dim, off)
        for at, half in enumerate(order):
            sem = fwd.at[0 if off == 1 else 1] if at == 0 else rest_sem
            begin, rows = halves(seg)[half]
            piece = view(mine + begin, rows)
            push(source(begin, rows) if source else piece, piece, send, sem, device)


def ring_forward(place, dim, view, rest, seg, send, fwd, rest_sem):
    for which, off, half in ((0, 1, 0), (1, 3, 1)):
        begin, rows = halves(seg)[half]
        piece = view(rest + place.at(dim, 4 - off) * seg + begin, rows)
        await_bytes(piece, fwd.at[which])
        push(piece, piece, send, rest_sem, place.near(dim, off))


def ring_end(like, send, rest_sem):
    await_bytes(like(2), rest_sem)
    await_bytes(like(3), send)


def pair_start(place, view, rest, seg, stride, transit, send, fwd, source=None):
    mine = rest + lax.div(place.pos["z"], 2) * stride
    for which, off in ((0, 1), (1, 3)):
        begin, rows = halves(seg)[which]
        piece = source(begin, rows) if source else view(mine + begin, rows)
        push(piece, transit.at[which, pl.ds(0, rows)], send, fwd.at[which], place.near("z", off))


def pair_forward(place, view, rest, seg, stride, transit, send, fwd, rest_sem):
    for which, off in ((0, 1), (1, 3)):
        begin, rows = halves(seg)[which]
        row = rest + lax.div(place.at("z", 4 - off), 2) * stride + begin
        piece = transit.at[which, pl.ds(0, rows)]
        await_bytes(piece, fwd.at[which])
        push(piece, view(row, rows), send, rest_sem, place.near("z", off))


def pair_end(like, send, rest_sem):
    await_bytes(like(1), rest_sem)
    await_bytes(like(2), send)


class Plan:
    LINK = 88e3
    CORES = 300e3
    MEMORY = 1500e3
    DELAY = 2.0
    LOCAL = 1.6
    PUSH = 0.04
    WAIT = 0.02
    SLOWER = 1.0

    def __init__(self):
        self.steps = []
        self.events = {}
        self.queues = {}
        self.now = 4.0
        self.trail = []

    def add(self, name, run, cost=0.0, after=(), needs=(), sends=(), rank=0.0, kind=0):
        cost = cost * self.SLOWER if kind == 1 else cost
        self.steps.append((name, run, cost, tuple(after), tuple(needs), tuple(sends), rank, kind))
        return name

    def send(self, event, link, size):
        if link == MEMORY:
            there = self.now + self.LOCAL + size / self.MEMORY
        else:
            taken = size / self.CORES if link == CORES else 2 * size / self.LINK
            begin = max(self.now + 0.3, self.queues.get(link, 0.0))
            self.queues[link] = begin + taken
            there = begin + taken + self.DELAY
        self.events[event] = max(self.events.get(event, 0.0), there)

    def order(self):
        left = list(self.steps)
        done = set()
        runs = []
        while left:
            best, best_key = None, None
            for at, (name, run, cost, after, needs, sends, rank, kind) in enumerate(left):
                if not all(other in done for other in after):
                    continue
                ready = max([self.events[event] for event in needs], default=0.0)
                late = ready > self.now
                key = (late, ready if late else 0.0, kind, rank, at)
                if best is None or key < best_key:
                    best, best_key = at, key
            name, run, cost, after, needs, sends, rank, kind = left.pop(best)
            self.now = max([self.now] + [self.events[event] for event in needs])
            for event, link, size in sends:
                self.now += self.PUSH
                self.send(event, link, size)
            self.now += cost + self.WAIT * len(needs)
            done.add(name)
            self.trail.append((name, round(self.now, 1)))
            runs.append(run)
        return runs


PACK, SHARE, WIDE, OPEN, FORWARD, FETCH, READY, GRAD, START, MIDDLE, END, FINISH, SMALLS, BEGIN, PASS, CLOSE = range(16)
LEAD, REST, SUM, STAGED, FIRST, LAST, ALL, ACROSS = range(20, 28)
MEMORY, CORES = range(2)
BOTH_WAYS = ((1, 0), (3, 1))


class Gather:
    RINGS = (("x", "y"), ("y", "x"))

    def __init__(self, refs, place, layers):
        self.__dict__.update(refs)
        self.place = place
        self.layers = layers
        self.shares = (
            place.pos["y"] * UNIT + place.pos["x"] * 48,
            place.pos["x"] * UNIT + place.pos["y"] * 48,
        )

    def view(self, b, g):
        def view(row, rows):
            return self.landed.at[b, g, lax.div(row, UNIT), pl.ds(m8(lax.rem(row, UNIT)), rows)]

        return view

    def share(self, b, g):
        n = 2 * b + g
        return self.pool.at[36 + n // 4, pl.ds(48 * (n % 4), 48)]

    def cross_share(self, b):
        own = self.layers.weight(BLOCKS[b][0], BLOCKS[b][1], 0)
        for g in range(2):
            row = pl.multiple_of(self.shares[g], 16)
            small = self.share(b, g)
            small[...] = own[pl.ds(row, 48), g * GW : (g + 1) * GW].astype(F32)
            for n, off in ((0, 1), (1, 3)):
                push(
                    small.at[pl.ds(24 * n, 24)],
                    self.view(b, g)(self.shares[g] + 24 * n, 24),
                    self.z_send.at[b, g],
                    self.z_recv.at[b, g],
                    self.place.near("z", off),
                )

    def cross_wide(self, b):
        own = self.layers.weight(BLOCKS[b][0], BLOCKS[b][1], 0)
        for r in range(4):
            for top in range(0, UNIT, 64):
                self.pool[4 * b + r, top : top + 64, :] = own[r * UNIT + top : r * UNIT + top + 64, 2 * GW :].astype(F32)
        for n, off in ((0, 1), (1, 3)):
            push(
                self.pool.at[pl.ds(4 * b + 2 * n, 2)],
                self.landed.at[b, 2, pl.ds(2 * n, 2)],
                self.z_send.at[b, 2],
                self.z_recv.at[b, 2],
                self.place.near("z", off),
            )

    def ring(self, b, g, at, part):
        dim = self.RINGS[g][at]
        seg = (48, UNIT)[at]
        rest = self.place.pos[self.RINGS[g][1]] * UNIT if at == 0 else 0
        view = self.view(b, g)
        send, fwd, rest_sem = self.ring_send.at[b, g, at], self.ring_fwd.at[b, g, at], self.ring_rest.at[b, g, at]
        if part == 0:
            ring_start(self.place, dim, view, rest, seg, send, fwd, rest_sem)
        elif part == 1:
            ring_forward(self.place, dim, view, rest, seg, send, fwd, rest_sem)
        elif at == 0:
            ring_end(lambda k: self.landed.at[b, g, 0, pl.ds(0, 48 * k)], send, rest_sem)
        else:
            ring_end(lambda k: self.landed.at[b, g, pl.ds(0, k)], send, rest_sem)

    def load(self, b, g):
        return pltpu.make_async_copy(self.landed.at[b, g], self.pool.at[pl.ds(24 + 4 * g, 4)], self.low_sem.at[g])

    def fetch(self, b, g):
        if g < 2:
            self.ring(b, g, 1, 2)
            self.load(b, g).start()
            await_bytes(self.share(b, g), self.z_send.at[b, g])
        else:
            await_bytes(self.landed.at[b, 2], self.z_recv.at[b, 2])
            self.load(b, g).start()
            await_bytes(self.landed.at[b, 2], self.z_send.at[b, 2])

    def convert(self, b, g):
        self.load(b, g).wait()

        @pl.loop(0, 4)
        def _(r):
            for top in range(0, UNIT, 64):
                rows = pl.ds(pl.multiple_of(r * UNIT + top, 64), 64)
                self.w[b, 1, rows, g * GW : (g + 1) * GW] = self.pool[24 + 4 * g + r, top : top + 64, :].astype(BF16)

    def ring_open(self, b, g, at):
        if at == 0:
            await_bytes(self.share(b, g), self.z_recv.at[b, g])
        else:
            self.ring(b, g, 0, 2)
        self.ring(b, g, at, 0)

    def schedule(self, plan):
        row = 4 * GW

        def z_both(event, size):
            return [(event, ("z", way), size) for way in (1, 3)]

        before = None
        for kind, b in [(kind, b) for kind in (SHARE, WIDE) for b in range(6)]:
            after = [(PACK, b // 3)] + ([before] if before else [])
            if kind == SHARE:
                sends = [send for g in range(2) for send in z_both((SHARE, b, g), 24 * row)]
                before = plan.add((SHARE, b), functools.partial(self.cross_share, b), 0.2, after, (), sends, 2.5)
            else:
                sends = z_both((WIDE, b), 384 * row)
                before = plan.add((WIDE, b), functools.partial(self.cross_wide, b), 0.5, after, (), sends, 2.5)
        for b in range(len(BLOCKS)):
            for g in range(2):
                previous = (SHARE, b)
                for at in range(2):
                    dim = self.RINGS[g][at]
                    half = (48, UNIT)[at] * row // 2
                    needs = [(SHARE, b, g)] if at == 0 else [(REST, b, g, 0)]
                    sends = []
                    for off, which in BOTH_WAYS:
                        sends += [((LEAD, b, g, at, which), (dim, off), half), ((REST, b, g, at), (dim, off), half)]
                    after = [previous]
                    if at and b:
                        after.append((FORWARD, b - 1, g, 1))
                    elif b > 1:
                        after.append((OPEN, b - 2, g, 1))
                    opened = plan.add((OPEN, b, g, at), functools.partial(self.ring_open, b, g, at), 0.0, after, needs, sends, b)
                    needs = [(LEAD, b, g, at, which) for which in range(2)]
                    sends = [((REST, b, g, at), (dim, off), half) for off, which in BOTH_WAYS]
                    run = functools.partial(self.ring, b, g, at, 1)
                    previous = plan.add((FORWARD, b, g, at), run, 0.0, [opened], needs, sends, b)
            for g in range(3):
                after = [(FORWARD, b, g, 1) if g < 2 else (WIDE, b)] + ([(READY, b - 1, g)] if b else [])
                needs = [(REST, b, g, 1)] if g < 2 else [(WIDE, b)]
                sends = [((FETCH, b, g), MEMORY, D * row)]
                fetched = plan.add((FETCH, b, g), functools.partial(self.fetch, b, g), 0.0, after, needs, sends, b)
                plan.add((READY, b, g), functools.partial(self.convert, b, g), 0.45, [fetched], [(FETCH, b, g)], (), b)


ROW_UP = 6
ROW_QKV = 8
SUBHEADS = SUBH // HEAD_DIM
QKV = 640
INV_ROOT_TAU = 0.3989422804014327


def dot(first_op, second_op):
    return jnp.dot(first_op, second_op, preferred_element_type=F32)


def dot_rows(first_op, second_op):
    return lax.dot_general(first_op, second_op, (((1,), (1,)), ((), ())), preferred_element_type=F32)


def row_sum(array):
    return jnp.sum(array, axis=0, keepdims=True)


class Layers:
    def __init__(self, refs, place, frames):
        self.__dict__.update(refs)
        self.place = place
        self.frames = frames
        self.sums = 0
        self.pending = {}
        self.waiting = {}
        self.stage_at = 0


    def weight(self, level, kind, s):
        b = 3 * level + KINDS.index(kind)
        if (b, s) in self.waiting:
            self.waiting.pop((b, s)).wait()
        return self.w.at[b, s]

    def attn_loads(self, level, w_query, w_key, w_value, w_out):
        low = pl.ds(0, 2 * SUBH)
        if level == 0:
            spots = [self.gt.at[1, 0, :, low], self.gt.at[1, 1, :, low], self.gt.at[0, 0, :, low]]
        else:
            spots = [self.gt.at[0, 1, :, low], self.h2t.at[0, :, low], self.h2t.at[1, :, low]]
        last = self.du.at[level, pl.ds(0, SUBH)]
        rows = pl.ds(pl.multiple_of(self.place.core * SUBH, 16), SUBH)
        sources = [w_query.at[level], w_key.at[level], w_value.at[level], w_out.at[level, rows]]
        return [pltpu.make_async_copy(a, b, self.attn_sem.at[level, n]) for n, (a, b) in enumerate(zip(sources, spots + [last]))]

    def attn_pack(self, level, copies):
        b = 3 * level
        for copy in copies:
            copy.wait()
        spots = [copy.dst_ref for copy in copies]
        for c in range(2):

            @pl.when(self.place.core == c)
            def _():
                def body(rows):
                    parts = [spot[rows, c * SUBH : (c + 1) * SUBH] for spot in spots[:3]]
                    self.w[b, 0, rows, : 3 * SUBH] = jnp.concatenate(parts, axis=1)

                rows_loop(D, 64, body)

        self.w[b, 0, :, 3 * SUBH :] = spots[3][...].T


    def sum_copy(self, n, c):
        rows = pl.ds(c * PAD, PAD)
        return remote(
            self.part.at[rows], self.land.at[n % 2, rows], self.sum_send.at[n, c], self.sum_recv.at[n, c], self.place.sibling()
        )

    def sum_start(self, n, c):
        self.sum_copy(n, c).start()

    def summed(self, n, c):
        self.sum_copy(n, c).wait()
        return lambda rows: self.part[rows, :] + self.land[n % 2, rows, :]

    def tile_loop(self, c, body, step=64):
        @pl.loop(0, PAD // step)
        def _(i):
            at = pl.multiple_of(i * step, step)
            body(pl.ds(pl.multiple_of(c * PAD + at, step), step), pl.ds(at, step))

    def vector(self, level, row):
        if row in (ROW_UP + 1, ROW_QKV + 1):
            at = 8 * level + (0 if row == ROW_UP + 1 else 1)
            return self.bias_other[at : at + 1, :]
        return self.vec[level, row : row + 1, :]

    @staticmethod
    def centred(x):
        c = x - jnp.mean(x, axis=-1, keepdims=True)
        return c, lax.rsqrt(jnp.mean(c * c, axis=-1, keepdims=True) + EPSILON)


    def f_attend(self, level, c, n_in):
        gain, shift = self.vector(level, 0), self.vector(level, 1)
        if level == 0:
            before = None
        else:
            before, b_down = self.summed(n_in, c), self.vector(level - 1, 5)

        def body(rows, at):
            if before is None:
                x = self.x[0, rows, :]
            else:
                x = self.mid[level - 1, rows, :] + before(rows) + b_down
                self.x[level, rows, :] = x
            centre, root = self.centred(x)
            self.hb[rows, :] = (centre * root * gain + shift).astype(BF16)

        self.tile_loop(c, body)
        rows = slice(c * PAD, (c + 1) * PAD)
        self.h1t[level, :, rows] = self.hb[rows, :].T

    def f_project(self, level, c, s):
        rows = slice(c * PAD, (c + 1) * PAD)
        h = self.hb[rows, :]
        wa = self.weight(level, "attn", s)
        bias = self.vector(level, ROW_QKV + s)
        for lo, hi in ((0, 256), (256, 512), (512, QKV)):
            value = (dot(h, wa[:, lo:hi]) + bias[:, lo:hi]).astype(BF16)
            if lo == 0:
                query = lax.broadcasted_iota(jnp.int32, (PAD, 256), 1) < SUBH
                value = jnp.where(query, value * HEAD_DIM**-0.5, value)
            self.qkv[level, s, rows, lo:hi] = value

    def f_mix(self, level, c, s):
        rows = slice(c * PAD, (c + 1) * PAD)
        block = self.qkv[level, s, rows, :]
        heads = [self.heads(block, head) for head in range(SUBHEADS)]
        scores = [self.masked(dot_rows(k, q)) for q, k, v in heads]
        tops = [jnp.max(score, axis=0, keepdims=True) for score in scores]
        exps = [jnp.exp(score - top) for score, top in zip(scores, tops)]
        totals = [row_sum(value) for value in exps]
        mixed = [dot(v.T, value.astype(BF16)) for (q, k, v), value in zip(heads, exps)]
        for head, (top, total) in enumerate(zip(tops, totals)):
            at = SUBHEADS * s + head
            self.lse[level, c, at : at + 1, :] = top + jnp.log(total)
        mixed = [jnp.zeros((HEAD_DIM, PAD), F32)] + [value * (1.0 / total) for value, total in zip(mixed, totals)]
        self.a[level, s, rows, :] = jnp.concatenate(mixed, axis=0).T.astype(BF16)

    def masked(self, scores):
        edge = self.frames // 8 * 8
        last = lax.broadcasted_iota(jnp.int32, (PAD - edge, PAD), 0) < self.frames - edge
        return jnp.concatenate([scores[:edge], jnp.where(last, scores[edge:], -1e30)], axis=0)

    def f_out(self, level, c, n_out):
        rows = slice(c * PAD, (c + 1) * PAD)
        for lo in range(0, D, GW):
            out = [dot_rows(self.a[level, s, rows, :], self.weight(level, "attn", s)[lo : lo + GW, 512:D]) for s in range(2)]
            self.part[rows, lo : lo + GW] = out[0] + out[1]
        self.sum_start(n_out, c)

    @staticmethod
    def heads(block, head):
        lo = head * HEAD_DIM
        return tuple(block[:, n * SUBH + lo : n * SUBH + lo + HEAD_DIM] for n in range(3))

    def f_up(self, level, c, n_in):
        gain, shift, b_out = self.vector(level, 2), self.vector(level, 3), self.vector(level, 4)
        branch = self.summed(n_in, c)

        def body(rows, at):
            x = self.x[level, rows, :] + branch(rows) + b_out
            self.mid[level, rows, :] = x
            centre, root = self.centred(x)
            self.hb[rows, :] = (centre * root * gain + shift).astype(BF16)

        self.tile_loop(c, body)
        rows = slice(c * PAD, (c + 1) * PAD)
        self.h2t[level, :, rows] = self.hb[rows, :].T

    def f_hidden(self, level, c, s):
        rows = slice(c * PAD, (c + 1) * PAD)
        h = self.hb[rows, :]
        wu = self.weight(level, "up", s)
        bias = self.vector(level, ROW_UP + s)
        for lo in range(0, SUB, GW):
            self.u[:, lo : lo + GW] = dot(h, wu[:, lo : lo + GW]) + bias[:, lo : lo + GW]

        def gelu(rows, at):
            u = self.u[at, :]
            half = 0.5 + 0.5 * lax.erf(u * HALF_ROOT)
            self.du[s, rows, :] = (u * half).astype(BF16)
            self.gp[level, s, rows, :] = (half + u * (jnp.exp(u * u * -0.5) * INV_ROOT_TAU)).astype(BF16)

        self.tile_loop(c, gelu, 32)
        self.gt[level, s, :, rows] = self.du[s, rows, :].T

    def f_down(self, level, c, n_out):
        rows = slice(c * PAD, (c + 1) * PAD)
        for lo in range(0, D, GW):
            out = [dot(self.du[s, rows, :], self.weight(level, "down", s)[:, lo : lo + GW]) for s in range(2)]
            self.part[rows, lo : lo + GW] = out[0] + out[1]
        self.sum_start(n_out, c)

    def f_end(self, n_in):
        for c in range(2):
            total = self.summed(n_in, c)

            @pl.when(self.place.core == c)
            def _():
                def body(rows, at):
                    self.u[at, :] = self.mid[LAYERS - 1, rows, :] + total(rows) + self.vector(LAYERS - 1, 5)

                self.tile_loop(c, body)


    def add_row(self, level, row, value):
        at = 12 * level + row
        self.small[at : at + 1, :] = self.small[at : at + 1, :] + value

    def norm_back(self, level, c, total, x_ref, gain_row, grad_row, after):
        gain = self.vector(level, gain_row)

        def body(rows, at):
            dh = total(rows)
            centre, root = self.centred(x_ref[level, rows, :])
            n = centre * root
            self.add_row(level, grad_row, row_sum(dh * n))
            self.add_row(level, grad_row + 1, row_sum(dh))
            dn = dh * gain
            shift = jnp.mean(dn, axis=-1, keepdims=True)
            slope = jnp.mean(dn * n, axis=-1, keepdims=True)
            dx = self.dx[rows, :] + root * (dn - shift - n * slope)
            self.dx[rows, :] = dx
            after(rows, at, dx)

        self.tile_loop(c, body)

    def b_low(self, level, c):
        def body(rows, at):
            dx = self.dx[rows, :]
            self.add_row(level, 5, row_sum(dx))
            self.dm[rows, :] = dx.astype(BF16)

        self.tile_loop(c, body)

    def b_hidden(self, level, c, s):
        rows = slice(c * PAD, (c + 1) * PAD)
        dm = self.dm[rows, :]
        wd = self.weight(level, "down", s)
        sums = []
        for lo in range(0, SUB, GW):
            dg = dot_rows(dm, wd[lo : lo + GW, :])
            du = (dg * self.gp[level, s, rows, lo : lo + GW].astype(F32)).astype(BF16)
            self.du[s, rows, lo : lo + GW] = du
            sums.append(row_sum(du.astype(F32)))
        self.add_row(level, ROW_UP + s, jnp.concatenate(sums, axis=1))

    def b_up(self, level, c, n_out):
        rows = slice(c * PAD, (c + 1) * PAD)
        for lo in range(0, D, GW):
            out = [dot_rows(self.du[s, rows, :], self.weight(level, "up", s)[lo : lo + GW, :]) for s in range(2)]
            self.part[rows, lo : lo + GW] = out[0] + out[1]
        self.sum_start(n_out, c)

    def stage_copy(self, slot, b, s, g):
        return pltpu.make_async_copy(self.staged.at[slot], self.grads.at[b, s, g], self.stage_sem.at[slot])

    def settle(self, b):
        for slot, key in list(self.pending.items()):
            if key[0] == b:
                self.stage_copy(slot, *key).wait()
                self.pending.pop(slot)

    def grad(self, key, s, left, right, extra=None):
        b = BACK_BLOCKS.index(key)
        for g in range(3):
            slot = self.stage_at % 4
            self.stage_at += 1
            if slot in self.pending:
                self.stage_copy(slot, *self.pending.pop(slot)).wait()
            value = dot(left[...], right[:, g * GW : (g + 1) * GW])
            if extra is not None and g == 2:
                value = value + dot(extra[0][...], extra[1][...])
            self.staged[slot] = value.reshape(4, UNIT, GW)
            self.stage_copy(slot, b, s, g).start()
            self.pending[slot] = (b, s, g)

    def b_grad_down(self, level, s):
        self.grad((level, "down"), s, self.gt.at[level, s], self.dm)

    def b_grad_up(self, level, s):
        self.grad((level, "up"), s, self.h2t.at[level], self.du.at[s])

    def b_grad_attn(self, level, s):
        self.grad((level, "attn"), s, self.h1t.at[level], self.du.at[s], (self.dbt, self.a.at[level, s]))

    def b_attend(self, level, c, n_in):
        total = self.summed(n_in, c)

        def after(rows, at, dx):
            self.add_row(level, 4, row_sum(dx))
            self.hb[rows, :] = dx.astype(BF16)

        self.norm_back(level, c, total, self.mid, 2, 2, after)
        rows = slice(c * PAD, (c + 1) * PAD)
        self.dbt[:, rows] = self.hb[rows, :].T

    def b_mix(self, level, c, s):
        rows = slice(c * PAD, (c + 1) * PAD)
        da = dot(self.hb[rows, :], self.weight(level, "attn", s)[:, 512:D]).astype(BF16)
        block = self.qkv[level, s, rows, :]
        heads = [self.heads(block, head) for head in range(SUBHEADS)]
        da_heads = [da[:, HEAD_DIM * (head + 1) : HEAD_DIM * (head + 2)] for head in range(SUBHEADS)]
        scores = [self.masked(dot_rows(k, q)) for q, k, v in heads]
        d_probs = [dot_rows(v, da_head) for (q, k, v), da_head in zip(heads, da_heads)]
        at = SUBHEADS * s
        probs = [jnp.exp(score - self.lse[level, c, at + head : at + head + 1, :]) for head, score in enumerate(scores)]
        dv = [dot(value.astype(BF16), da_head).astype(BF16) for value, da_head in zip(probs, da_heads)]
        d_scores = [(p * (dp - row_sum(p * dp))).astype(BF16) for p, dp in zip(probs, d_probs)]
        dk = [dot(value, q).astype(BF16) for (q, k, v), value in zip(heads, d_scores)]
        dq = [dot(k.T, value) * HEAD_DIM**-0.5 for (q, k, v), value in zip(heads, d_scores)]
        d_query = jnp.concatenate(dq, axis=0).T.astype(BF16)
        zeros = jnp.zeros((PAD, D - 3 * SUBH), BF16)
        block = jnp.concatenate([d_query] + dk + dv + [zeros], axis=1)
        self.du[s, rows, :] = block
        self.add_row(level, ROW_QKV + s, row_sum(block.astype(F32)))

    def b_in(self, level, c, n_out):
        rows = slice(c * PAD, (c + 1) * PAD)
        for lo in range(0, D, GW):
            out = [
                dot_rows(self.du[s, rows, :QKV], self.weight(level, "attn", s)[lo : lo + GW, :QKV]) for s in range(2)
            ]
            self.part[rows, lo : lo + GW] = out[0] + out[1]
        self.sum_start(n_out, c)

    def b_first(self, level, c, n_in):
        total = self.summed(n_in, c)

        def after(rows, at, dx):
            if level > 0:
                self.add_row(level - 1, 5, row_sum(dx))
                self.dm[rows, :] = dx.astype(BF16)

        self.norm_back(level, c, total, self.x, 0, 0, after)

    def schedule(self, plan, pack, take_cot, leave_act, finish):
        last = LAYERS - 1
        clip_bytes = 4 * PAD * D
        chain = []

        def add(run, cost, *args, name=None, after=(), needs=(), sends=()):
            name = name or (-1, len(chain))
            chain.append(plan.add(name, functools.partial(run, *args), cost, list(after) + chain[-1:], needs, sends, 0.0, 1))

        def ready(level, kind):
            b = 3 * level + KINDS.index(kind)
            return [(READY, b, g) for g in range(3)]

        def summing(n, c):
            return [((SUM, n, c), CORES, clip_bytes)]

        def staging(level, kind):
            return [((STAGED, BACK_BLOCKS.index((level, kind))), MEMORY, 4 * D * D)]

        def grad(run, cost, level, kind):
            for s in range(2):
                add(run, cost, level, s, name=(GRAD, level, kind, s), sends=staging(level, kind))

        add(pack, 1.0, 0, name=(PACK, 0))
        add(pack, 1.0, 1, name=(PACK, 1))
        n = 0
        for level in range(LAYERS):
            for c in range(2):
                add(self.f_attend, 0.7, level, c, n - 1, needs=[(SUM, n - 1, c)] if level else ())
                add(self.f_project, 0.4, level, c, 0)
                add(self.f_mix, 1.6, level, c, 0)
            if level == 0:
                add(take_cot, 0.1)
                for c in range(2):
                    add(self.b_low, 0.3, last, c)
            for c in range(2):
                add(self.f_project, 0.4, level, c, 1, after=ready(level, "attn"))
                add(self.f_mix, 1.6, level, c, 1)
                add(self.f_out, 0.5, level, c, n, sends=summing(n, c))
            for c in range(2):
                add(self.f_up, 0.8, level, c, n, needs=[(SUM, n, c)])
                add(self.f_hidden, 1.4, level, c, 0)
            for c in range(2):
                add(self.f_hidden, 1.4, level, c, 1, after=ready(level, "up"))
                if level < last:
                    add(self.f_down, 0.7, level, c, n + 1, after=ready(level, "down"), sends=summing(n + 1, c))
            n += 2
        grad(self.b_grad_down, 1.1, last, "down")
        for c in range(2):
            add(self.f_down, 0.7, last, c, n - 1, after=ready(last, "down"), sends=summing(n - 1, c))
        for level in reversed(range(LAYERS)):
            for c in range(2):
                if level < last:
                    add(self.b_first, 1.0, level + 1, c, n - 1, needs=[(SUM, n - 1, c)])
                for s in range(2):
                    add(self.b_hidden, 0.7, level, c, s)
                if level == last and c == 0:
                    add(self.f_end, 0.5, n - 1, needs=[(SUM, n - 1, 0), (SUM, n - 1, 1)])
                    add(leave_act, 0.1, sends=[((ACROSS, 0), ("z", 1), clip_bytes)])
                add(self.b_up, 0.7, level, c, n, sends=summing(n, c))
            if level < last:
                grad(self.b_grad_down, 1.1, level, "down")
            grad(self.b_grad_up, 1.1, level, "up")
            for c in range(2):
                add(self.b_attend, 1.2, level, c, n, needs=[(SUM, n, c)])
                for s in range(2):
                    add(self.b_mix, 2.4, level, c, s)
                add(self.b_in, 0.8, level, c, n + 1, sends=summing(n + 1, c))
            grad(self.b_grad_attn, 1.4, level, "attn")
            n += 2
        for c in range(2):
            add(self.b_first, 1.0, 0, c, n - 1, needs=[(SUM, n - 1, c)])
        add(finish, 0.5, name=(FINISH, 0), sends=[((ACROSS, 1), ("z", 1), clip_bytes)])


COMPUTE_SCRATCH = dict(
    w=((len(BLOCKS), 2, D, D), BF16),
    x=((LAYERS, 2 * PAD, D), F32),
    mid=((LAYERS, 2 * PAD, D), F32),
    dx=((2 * PAD, D), F32),
    part=((2 * PAD, D), F32),
    land=((2, 2 * PAD, D), F32),
    h1t=((LAYERS, D, 2 * PAD), BF16),
    h2t=((LAYERS, D, 2 * PAD), BF16),
    qkv=((LAYERS, 2, 2 * PAD, QKV), BF16),
    a=((LAYERS, 2, 2 * PAD, 256), BF16),
    lse=((LAYERS, 2, 8, PAD), F32),
    gt=((LAYERS, 2, SUB, 2 * PAD), BF16),
    gp=((LAYERS, 2, 2 * PAD, SUB), BF16),
    hb=((2 * PAD, D), BF16),
    u=((PAD, SUB), F32),
    dm=((2 * PAD, D), BF16),
    du=((2, 2 * PAD, SUB), BF16),
    dbt=((D, 2 * PAD), BF16),
    staged=((4, 4, UNIT, GW), F32),
    small=((SMALL_ROWS, D), F32),
    small_all=((3, 4, SMALL_ROWS, D), F32),
    sum_three=((6, 3, 24, GW), F32),
    bias_other=((8 * LAYERS, D), F32),
    bias_own=((8 * LAYERS, D), F32),
    vec=((LAYERS, 16, D), F32),
    pool=((48, UNIT, GW), F32),
    first_two=((3, 2, 3, 48, GW), F32),
    last_two=((3, 4, 3, 48, GW), F32),
    sum_two=((3, 2, 3, 48, GW), F32),
    heard_three=((3, 6, 6, 24, 128), F32),
)
SUMS = 4 * LAYERS


class Reduce:
    BUNDLES = ((0, 1), (1, 1), (2, 1), (3, 2), (5, 1))

    def __init__(self, refs, place, layers):
        self.__dict__.update(refs)
        self.place = place
        self.layers = layers


    def span(self, n, phase):
        return (n, 1) if phase == 0 else self.BUNDLES[n]

    def holder(self, b):
        return next(n for n, (first, count) in enumerate(self.BUNDLES) if first <= b - 3 < first + count)

    def slot(self, n):
        return self.BUNDLES[n][0] % 3

    def order(self, n, phase):
        return ORDERS[self.span(n, phase)[0] // 3]

    def set_of(self, z):
        return lax.rem(lax.rem(z, 2) + self.place.t, 2)

    def unit(self, n, g, phase, chunk, part):
        first, count = self.span(n, phase)
        low, high = lax.rem(chunk, 2), lax.div(chunk, 2)
        if phase == 0:
            which, row = (part, chunk) if g < 2 else (self.set_of(chunk), 2 * high + part)
            return self.grads.at[n, which, g, row]
        if phase == 1:
            if g == 0:
                which, row = part, chunk * 48
            elif g == 1:
                which, row = self.set_of(chunk), high * 96 + part * 48
            else:
                which, row = high, low * 96 + part * 48
            return self.pool.at[pl.ds(30 + (2 * g + which) * 3 + self.slot(n), count), pl.ds(m8(row), 48)]
        which, row = (self.set_of(chunk), high) if g == 0 else (high, low)
        return self.sum_two.at[g, which, pl.ds(self.slot(n), count), pl.ds(m8(row * 24), 24), pl.ds(128 * part, 128)]

    def result(self, n, g, phase, part):
        first, count = self.span(n, phase)
        if phase == 0:
            return self.pool.at[30 + (2 * g + part) * 3 + n % 3]
        if phase == 1:
            return self.sum_two.at[g, part, pl.ds(self.slot(n), count)]
        return self.sum_three.at[pl.ds(first, count), g, :, pl.ds(128 * part, 128)]

    def heard(self, n, g, phase, slots):
        first, count = self.span(n, phase)
        if phase == 0:
            return self.heard_one.at[g, slots, n]
        return (self.heard_two, self.heard_three)[phase - 1].at[g, slots, pl.ds(first, count)]

    def pool_part(self, base, slots):
        if isinstance(slots, int):
            return self.pool.at[base + slots]
        return self.pool.at[pl.ds(base + slots.start, slots.size)]

    def first_box(self, n, g, phase, parts):
        count = self.span(n, phase)[1]
        if phase == 0:
            return self.pool_part(6 + 6 * (n % 2) + 2 * g, parts)
        if phase == 1:
            return self.first_two.at[g, parts, pl.ds(0, count)]
        return self.heard(n, g, phase, parts)

    def last_box(self, n, g, phase, slots):
        count = self.span(n, phase)[1]
        if phase == 0:
            return self.pool_part(18 + 4 * g, slots)
        if phase == 1:
            return self.last_two.at[g, slots, pl.ds(0, count)]
        if isinstance(slots, int):
            return self.heard(n, g, phase, slots + 2)
        return self.heard(n, g, phase, pl.ds(2, 4))

    def blocks(self, n, phase, *refs):
        if phase == 0:
            return [refs]
        return [tuple(ref.at[block] for ref in refs) for block in range(self.span(n, phase)[1])]

    def rs_start(self, n, g, phase):
        place = self.place
        if phase == 0:
            self.layers.settle(n)
        dim = self.order(n, phase)[g][phase]
        send, first, rest = self.rs_send.at[n, g, phase], self.rs_first.at[n, g, phase], self.rs_rest.at[n, g, phase]
        far = place.at(dim, 2)
        right, left = place.near(dim, 1), place.near(dim, 3)

        def out(chunk, part, slot, sem, device):
            unit = self.unit(n, g, phase, chunk, part)
            push(unit, self.heard(n, g, phase, slot), send, sem, device)

        out(far, 0, 0, first, right)
        out(far, 1, 1, first, left)
        out(place.at(dim, 1), 1, 3, rest, right)
        out(place.at(dim, 3), 0, 4, rest, left)

    def side_load(self, n, g, part):
        source = self.unit(n, g, 0, self.place.at(self.order(n, 0)[g][0], 1 if part == 0 else 3), part)
        return pltpu.make_async_copy(source, self.pool.at[2 * g + part], self.side_sem.at[g])

    def first_load(self, n, g, phase):
        both = pl.ds(0, 2)
        source, target = self.heard(n, g, phase, both), self.first_box(n, g, phase, both)
        return pltpu.make_async_copy(source, target, self.middle_sem.at[phase, g])

    def rs_middle_load(self, n, g, phase):
        if phase == 0:
            for part in range(2):
                self.side_load(n, g, part).start()
        await_bytes(self.heard(n, g, phase, pl.ds(0, 2)), self.rs_first.at[n, g, phase])
        self.first_load(n, g, phase).start()

    def rs_middle(self, n, g, phase):
        place = self.place
        dim = self.order(n, phase)[g][phase]
        if phase < 2:
            self.first_load(n, g, phase).wait()
        else:
            await_bytes(self.heard(n, g, phase, pl.ds(0, 2)), self.rs_first.at[n, g, phase])
        if phase == 0:
            await_bytes(self.pool.at[pl.ds(2 * g, 2)], self.side_sem.at[g])
        for part, off, slot in ((0, 1, 2), (1, 3, 5)):
            mine = self.first_box(n, g, phase, part)
            side = self.pool.at[2 * g + part] if phase == 0 else self.unit(n, g, phase, place.at(dim, off), part)
            for total, add in self.blocks(n, phase, mine, side):

                def body(rows):
                    total[rows, :] = total[rows, :] + add[rows, :]

                rows_loop(total.shape[0], 96, body)
            push(mine, self.heard(n, g, phase, slot), self.rs_send.at[n, g, phase], self.rs_rest.at[n, g, phase], place.near(dim, off))

    def last_load(self, n, g, phase):
        source, target = self.heard(n, g, phase, pl.ds(2, 4)), self.last_box(n, g, phase, pl.ds(0, 4))
        return pltpu.make_async_copy(source, target, self.end_sem.at[phase, g])

    def rs_end_load(self, n, g, phase):
        if phase == 0:
            for part in range(2):
                source = self.unit(n, g, 0, self.place.pos[self.order(n, 0)[g][0]], part)
                pltpu.make_async_copy(source, self.result(n, g, 0, part), self.mine_sem.at[g]).start()
        await_bytes(self.heard(n, g, phase, pl.ds(2, 4)), self.rs_rest.at[n, g, phase])
        self.last_load(n, g, phase).start()

    def rs_end(self, n, g, phase):
        if phase < 2:
            self.last_load(n, g, phase).wait()
        else:
            await_bytes(self.heard(n, g, phase, pl.ds(2, 4)), self.rs_rest.at[n, g, phase])
        if phase == 0:
            await_bytes(self.pool.at[pl.ds(30, 2)], self.mine_sem.at[g])
        for part in range(2):
            results = self.result(n, g, phase, part)
            own = results if phase == 0 else self.unit(n, g, phase, self.place.pos[self.order(n, phase)[g][phase]], part)
            lows, highs = self.last_box(n, g, phase, part), self.last_box(n, g, phase, 2 + part)
            for out, start, low, high in self.blocks(n, phase, results, own, lows, highs):

                def body(rows):
                    out[rows, :] = start[rows, :] + (low[rows, :] + high[rows, :])

                rows_loop(out.shape[0], 96, body)
        await_bytes(self.heard(n, g, phase, pl.ds(0, 6)), self.rs_send.at[n, g, phase])
        if phase == 1:
            self.rs_start(n, g, 2)

    def schedule(self, plan):
        units = [4 * UNIT * GW, 4 * 48 * GW, 4 * 24 * 128]

        def add(name, run, *args, cost=0.0, after=(), needs=(), sends=()):
            after = [step for step in after if step[1] >= 0]
            rank = 0.001 * (name[1] if name[3] == 0 else self.BUNDLES[name[1]][0])
            return plan.add(name, functools.partial(run, *name[1:3], *args), cost, after, needs, sends, rank)

        def opening(n, g, phase):
            dim, size = self.order(n, phase)[g][phase], units[phase] * self.span(n, phase)[1]
            sends = [((FIRST, n, g, phase), (dim, off), size) for off, _ in BOTH_WAYS]
            return sends + [((LAST, n, g, phase), (dim, off), size) for off, _ in BOTH_WAYS]

        def rest(n, g, phase, after):
            dim, size = self.order(n, phase)[g][phase], units[phase] * self.span(n, phase)[1]
            heard = (FIRST, n, g, phase)
            if phase < 2:
                pool = [(READY, b, part) for b in range(len(BLOCKS)) for part in range(3)]
                hold = pool + [(MIDDLE, n - 1, g, 0), (END, n - 2, g, 0)] if phase == 0 else [(END, n - 1, g, 1)]
                loads = [((MIDDLE, n, g, phase), MEMORY, size)] * (3 if phase == 0 else 1)
                after = [add((OPEN, n, g, phase, MIDDLE), self.rs_middle_load, phase, after=after + hold, needs=[heard], sends=loads)]
                heard = (MIDDLE, n, g, phase)
            sends = [((LAST, n, g, phase), (dim, off), size) for off, _ in BOTH_WAYS]
            after = [add((MIDDLE, n, g, phase), self.rs_middle, phase, cost=2e-6 * size, after=after, needs=[heard], sends=sends)]
            heard = (LAST, n, g, phase)
            if phase < 2:
                hold = [(END, n - 1, g, phase)] + ([(END, self.holder(n), g, 1)] if phase == 0 and n >= 3 else [])
                loads = [((END, n, g, phase), MEMORY, 2 * size)] * (3 if phase == 0 else 1)
                after = [add((OPEN, n, g, phase, END), self.rs_end_load, phase, after=after + hold, needs=[heard], sends=loads)]
                heard = (END, n, g, phase)
            if phase == 1:
                first, count = self.BUNDLES[n]
                after = after + [(END, self.holder(b), g, 2) for b in range(max(first, 3), first + count)]
            sends = opening(n, g, 2) if phase == 1 else ()
            return [add((END, n, g, phase), self.rs_end, phase, cost=3e-6 * size, after=after, needs=[heard], sends=sends)]

        for g in range(3):
            for b, (level, kind) in enumerate(BACK_BLOCKS):
                grads = [(GRAD, level, kind, s) for s in range(2)]
                rest(b, g, 0, [add((START, b, g, 0), self.rs_start, 0, after=grads, needs=[(STAGED, b)], sends=opening(b, g, 0))])
            for n, (first, count) in enumerate(self.BUNDLES):
                ready = [(END, b, g, 0) for b in range(first, first + count)]
                after = rest(n, g, 1, [add((START, n, g, 1), self.rs_start, 1, after=ready, sends=opening(n, g, 1))])
                rest(n, g, 2, after)


class Spread:
    EARLY_Z = (0, 1, 2, 3, 4)

    def __init__(self, refs, place):
        self.__dict__.update(refs)
        self.place = place

    def view(self, b, g):
        level, kind = BACK_BLOCKS[b]
        core = self.place.core
        columns = pl.ds(g * GW, GW)
        if kind == "up":
            return lambda row, rows: self.out_up.at[level, pl.ds(m8(row), rows), pl.ds(pl.multiple_of(core * SUB + g * GW, 128), GW)]
        if kind == "down":
            return lambda row, rows: self.out_down.at[level, pl.ds(m8(core * SUB + row), rows), columns]
        return lambda row, rows: self.out_attn.at[level, core, g, pl.ds(m8(row), rows)]

    def own_copy(self, b, g):
        phase, seg, _ = self.route(b, g)[0]
        row = self.spots(b, g, 0)[0] + self.where(ORDERS[b // 3][g][phase]) * seg
        return pltpu.make_async_copy(self.sum_three.at[b, g], self.view(b, g)(row, seg), self.own_sem.at[b, g])

    def where(self, dim):
        return lax.div(self.place.pos["z"], 2) if dim == "z" else self.place.pos[dim]

    @staticmethod
    def route(b, g):
        strides = STRIDES[g]
        if g == 2 and b in Spread.EARLY_Z:
            return ((2, strides[2], 1), (0, strides[1], 1), (1, strides[1], 2))
        return tuple((phase, strides[phase], 1) for phase in (2, 1, 0))

    def spots(self, b, g, step):
        route = self.route(b, g)
        done = {phase for phase, _, _ in route[: step + 1]}
        row = 0
        for n in range(3):
            if n not in done:
                row = row + self.where(ORDERS[b // 3][g][n]) * STRIDES[g][n]
        return [row + part * STRIDES[g][0] for part in range(route[step][2])]

    def ag(self, b, g, step, part):
        phase, seg, count = self.route(b, g)[step]
        dim = ORDERS[b // 3][g][phase]
        view = self.view(b, g)
        like = lambda k: view(0, k * seg)
        transit = (self.transit_0, self.transit_1, self.transit_2)[g].at[b] if dim == "z" else None
        for n, rest in enumerate(self.spots(b, g, step)):
            send, fwd, rest_sem = (array.at[b, g, step, n] for array in (self.ag_send, self.ag_fwd, self.ag_rest))
            if part == 0:
                source = None
                if step == 0:
                    self.own_copy(b, g).start()
                    source = lambda row, rows: self.sum_three.at[b, g, pl.ds(row, rows)]
                if dim == "z":
                    pair_start(self.place, view, rest, seg, STRIDES[g][phase], transit, send, fwd, source)
                else:
                    ring_start(self.place, dim, view, rest, seg, send, fwd, rest_sem, source)
            elif part == 1:
                if dim == "z":
                    pair_forward(self.place, view, rest, seg, STRIDES[g][phase], transit, send, fwd, rest_sem)
                else:
                    ring_forward(self.place, dim, view, rest, seg, send, fwd, rest_sem)
            elif dim == "z":
                pair_end(like, send, rest_sem)
            else:
                ring_end(like, send, rest_sem)

    def start(self, b, g):
        self.ag(b, g, 0, 0)

    def last(self, b, g):
        phase, seg, count = self.route(b, g)[2]
        return ORDERS[b // 3][g][phase], seg, self.spots(b, g, 2)

    def forward(self, b, g, step):
        self.ag(b, g, step, 1)
        dim, seg, rests = self.last(b, g)
        if step == 2 and dim != "z":
            for rest in rests:
                self.across(b, g, rest + self.place.at(dim, 3) * seg, halves(seg)[0])
                self.across(b, g, rest + self.place.at(dim, 1) * seg, halves(seg)[1])

    def end(self, b, g, step):
        self.ag(b, g, step, 2)
        if step == 0:
            self.own_copy(b, g).wait()
        dim, seg, rests = self.last(b, g)
        if step < 2:
            self.ag(b, g, step + 1, 0)
            if step == 1:
                for rest in rests:
                    self.across(b, g, rest + self.where(dim) * seg, (0, seg))
            return
        for rest in rests:
            if dim == "z":
                self.across(b, g, rest + (1 - self.where(dim)) * seg, (0, seg))
            else:
                self.across(b, g, rest + self.place.at(dim, 3) * seg, halves(seg)[1])
                self.across(b, g, rest + self.place.at(dim, 1) * seg, halves(seg)[0])
                self.across(b, g, rest + self.place.at(dim, 2) * seg, (0, seg))

    def across(self, b, g, row, span):
        piece = self.view(b, g)(row + span[0], span[1])
        push(piece, piece, self.d2d_send.at[b, g], self.d2d_recv.at[b, g], self.place.sibling())

    def across_end(self, b, g):
        whole = self.view(b, g)(0, D)
        remote(whole, whole, self.d2d_send.at[b, g], self.d2d_recv.at[b, g], self.place.sibling()).wait()


    def small_start(self, n):
        dim = "xyz"[n]
        mine = self.small_all.at[n, self.place.pos[dim]]
        mine[...] = self.small[...]
        for off in (1, 2, 3):
            push(mine, mine, self.misc_send.at[3 + n], self.misc_recv.at[3 + n], self.place.near(dim, off))

    def small_end(self, n):
        await_bytes(self.small_all.at[n, pl.ds(0, 3)], self.misc_recv.at[3 + n])
        await_bytes(self.small_all.at[n, pl.ds(0, 3)], self.misc_send.at[3 + n])
        self.small[...] = (self.small_all[n, 0] + self.small_all[n, 1]) + (self.small_all[n, 2] + self.small_all[n, 3])

    def small_copy(self):
        return remote(
            self.small, self.small_both.at[self.place.core], self.misc_send.at[6], self.misc_recv.at[6], self.place.sibling()
        )

    def small_share(self):
        self.small_both[self.place.core] = self.small[...]
        self.small_copy().start()

    def schedule(self, plan):
        before = [(FINISH, 0)]
        for n in range(3):
            sends = [((SMALLS, n), ("xyz"[n], off), 8 * SMALL_ROWS * D) for off in (1, 3)]
            before = [plan.add((SMALLS, n, 0), functools.partial(self.small_start, n), 0.1, before, (), sends, -1.0)]
            before = [plan.add((SMALLS, n, 1), functools.partial(self.small_end, n), 0.1, before, [(SMALLS, n)], (), -1.0)]
        plan.add((SMALLS, 3, 0), self.small_share, 0.1, before)
        for n, (first, count) in enumerate(Reduce.BUNDLES):
            for b, g in ((b, g) for b in range(first, first + count) for g in range(3)):

                def add(name, run, *args, after=(), needs=(), sends=()):
                    return plan.add(name, functools.partial(run, b, g, *args), 0.0, after, needs, sends, 0.001 * b, 2 if b else 0)

                route = self.route(b, g)

                def gathering(step):
                    phase, seg, count = route[step]
                    dim, half = ORDERS[b // 3][g][phase], seg * 512
                    sends = []
                    for off, which in BOTH_WAYS:
                        sends += [((LEAD, b, g, step, which), (dim, off), half)] * count
                        if dim != "z":
                            sends += [((ALL, b, g, step), (dim, off), half)] * count
                    return sends

                after = [add((BEGIN, b, g), self.start, after=[(END, n, g, 2)], sends=gathering(0))]
                for step, (phase, seg, count) in enumerate(route):
                    dim, half = ORDERS[b // 3][g][phase], seg * 512
                    lead = [(LEAD, b, g, step, which) for which in range(2)]
                    sends = [((ALL, b, g, step), (dim, off), half) for off, _ in BOTH_WAYS] * count
                    if step == 2 and dim != "z":
                        sends += [((ACROSS, b, g), CORES, half)] * 2 * count
                    after = [add((PASS, b, g, step), self.forward, step, after=after, needs=lead, sends=sends)]
                    if step < 2:
                        sends = gathering(step + 1)
                        if step == 1:
                            sends += [((ACROSS, b, g), CORES, route[2][1] * 1024)] * route[2][2]
                        if step == 1 and b and ORDERS[b // 3][g][route[2][0]] != "z":
                            after = after + [(PASS, b - 1, g, 2)]
                    else:
                        sends = [((ACROSS, b, g), CORES, half * 2)] * (1 if dim == "z" else 2 * count)
                    after = [add((CLOSE, b, g, step), self.end, step, after=after, needs=[(ALL, b, g, step)], sends=sends)]
                add((ACROSS, b, g), self.across_end, after=after + [(FINISH, 0)], needs=[(ACROSS, b, g)])


DMA_ARRAYS = dict(
    sum_send=(SUMS, 2),
    sum_recv=(SUMS, 2),
    w_sem=(len(BLOCKS), 2),
    x_sem=(4,),
    attn_sem=(LAYERS, 4),
    stage_sem=(4,),
    out_sem=(2,),
    z_send=(len(BLOCKS), 3),
    z_recv=(len(BLOCKS), 3),
    ring_send=(len(BLOCKS), 2, 2),
    ring_fwd=(len(BLOCKS), 2, 2, 2),
    ring_rest=(len(BLOCKS), 2, 2),
    low_sem=(3,),
    side_sem=(3,),
    middle_sem=(2, 3),
    end_sem=(2, 3),
    mine_sem=(3,),
    rs_send=(len(BLOCKS), 3, 3),
    rs_first=(len(BLOCKS), 3, 3),
    rs_rest=(len(BLOCKS), 3, 3),
    misc_send=(7,),
    misc_recv=(7,),
    ag_send=(len(BLOCKS), 3, 3, 2),
    ag_fwd=(len(BLOCKS), 3, 3, 2, 2),
    ag_rest=(len(BLOCKS), 3, 3, 2),
    own_sem=(len(BLOCKS), 3),
    d2d_send=(len(BLOCKS), 3),
    d2d_recv=(len(BLOCKS), 3),
)
HBM_ARRAYS = dict(
    out_up=(LAYERS, D, 2 * SUB),
    out_down=(LAYERS, 2 * SUB, D),
    out_attn=(LAYERS, 2, 3, D, GW),
    pair_own=(2, PAD, D),
    pair_far=(2, PAD, D),
    grads=(len(BLOCKS), 2, 3, 4, UNIT, GW),
    landed=(len(BLOCKS), 3, 4, UNIT, GW),
    heard_one=(3, 6, len(BLOCKS), UNIT, GW),
    heard_two=(3, 6, len(BLOCKS), 48, GW),
    transit_0=(len(BLOCKS), 2, 16, GW),
    transit_1=(len(BLOCKS), 2, 48, GW),
    transit_2=(len(BLOCKS), 2, 192, GW),
)


def step_kernel(frames, x_in, cot_in, w_query, w_key, w_value, w_out, up_own, down_own, *rest):
    place = Place()
    core, t = place.core, place.t
    vectors, rest = rest[:9], rest[9:]
    names = ["small_both"] + list(HBM_ARRAYS) + list(COMPUTE_SCRATCH) + list(DMA_ARRAYS)
    refs = dict(zip(names, rest))
    vec, bias_own = refs["vec"], refs["bias_own"]
    run = Layers(refs, place, frames)
    gather = Gather(refs, place, run)
    reduce = Reduce(refs, place, run)
    misc_send, misc_recv = refs["misc_send"], refs["misc_recv"]
    columns = pl.ds(pl.multiple_of(core * SUB, 128), SUB)
    rows = pl.ds(pl.multiple_of(core * SUB, 16), SUB)
    mine = pl.ds(pl.multiple_of(core * PAD, PAD), PAD)
    attn_loads = [run.attn_loads(level, w_query, w_key, w_value, w_out) for level in range(LAYERS)]
    for b, (level, kind) in enumerate(BLOCKS):
        if kind == "attn":
            for copy in attn_loads[level]:
                copy.start()
            continue
        source = up_own.at[level, :, columns] if kind == "up" else down_own.at[level, rows, :]
        run.waiting[b, 0] = pltpu.make_async_copy(source, run.w.at[b, 0], run.w_sem.at[b, 0])
        run.waiting[b, 0].start()
    clips = (x_in.at[t], cot_in.at[t])
    local = [
        pltpu.make_async_copy(clips[0], run.x.at[0, mine], run.x_sem.at[0]),
        pltpu.make_async_copy(clips[1], run.dx.at[mine], run.x_sem.at[1]),
    ]
    for copy in local:
        copy.start()

    for n in range(ROW_UP):
        vec[:, n, :] = vectors[n][...].astype(F32)
    query_bias, value_bias, up_bias = (vector[...].astype(F32) for vector in vectors[ROW_UP:])
    for c in range(2):

        @pl.when(core == c)
        def _():
            span = slice(c * SUBH, (c + 1) * SUBH)
            nothing = jnp.zeros((LAYERS, SUBH), F32)
            rows_up = up_bias[:, c * SUB : (c + 1) * SUB]
            rows_qkv = jnp.concatenate([query_bias[:, span], nothing, value_bias[:, span], nothing], axis=1)
            for level in range(LAYERS):
                line = slice(level, level + 1)
                for row, value in ((0, rows_up), (1, rows_qkv)):
                    bias_own[8 * level + row : 8 * level + row + 1, :] = value[line]
                vec[level, ROW_UP : ROW_UP + 1, :] = rows_up[line]
                vec[level, ROW_QKV : ROW_QKV + 1, :] = rows_qkv[line]

    greet([place.near(d, o) for d in "xyz" for o in (1, 2, 3)] + [place.sibling()])
    given = [
        remote(clips[0], run.x.at[0, mine], misc_send.at[0], misc_recv.at[0], place.sibling()),
        remote(bias_own, run.bias_other, misc_send.at[1], misc_recv.at[1], place.partner()),
        remote(clips[1], run.dx.at[mine], misc_send.at[2], misc_recv.at[2], place.sibling()),
    ]
    for copy in given:
        copy.start()

    run.small[...] = jnp.zeros_like(run.small)
    outs = [
        pltpu.make_async_copy(run.u, refs["pair_own"].at[0], run.out_sem.at[0]),
        pltpu.make_async_copy(run.dx.at[mine], refs["pair_own"].at[1], run.out_sem.at[1]),
    ]
    far = [
        remote(run.u, refs["pair_far"].at[0], misc_send.at[0], misc_recv.at[0], place.partner()),
        remote(run.dx.at[mine], refs["pair_far"].at[1], misc_send.at[1], misc_recv.at[1], place.partner()),
    ]

    def pack(level):
        run.attn_pack(level, attn_loads[level])
        if level == LAYERS - 1:
            local[0].wait()
            given[0].wait()
            given[1].wait()

    def take_cot():
        local[1].wait()
        given[2].wait()

    def leave_act():
        outs[0].start()
        far[0].start()

    def leave():
        outs[1].start()
        far[1].start()
        for level in range(LAYERS):
            for base in (ROW_UP, ROW_QKV):
                at = 12 * level + base
                pair = run.small[at : at + 2, :]
                swapped = jnp.concatenate([pair[1:2], pair[0:1]], axis=0)
                run.small[at : at + 2, :] = jnp.where(t == 0, pair, swapped)

    plan = Plan()
    run.schedule(plan, pack, take_cot, leave_act, leave)
    gather.schedule(plan)
    reduce.schedule(plan)
    spread = Spread(refs, place)
    spread.schedule(plan)
    for write in plan.order():
        write()
    spread.small_copy().wait()
    for copy in outs + far:
        copy.wait()


def step(frames, x, cot, weights, vectors):
    anywhere = pl.BlockSpec(memory_space=pl.ANY)
    vmem = pl.BlockSpec(memory_space=pltpu.VMEM)
    return pl.pallas_call(
        functools.partial(step_kernel, frames),
        out_shape=tuple(
            jax.ShapeDtypeStruct(shape, F32) for shape in ((2, SMALL_ROWS, D), *HBM_ARRAYS.values())
        ),
        in_specs=[anywhere] * 8 + [vmem] * len(vectors),
        out_specs=(vmem,) + (anywhere,) * len(HBM_ARRAYS),
        scratch_shapes=[pltpu.VMEM(*spec) for spec in COMPUTE_SCRATCH.values()]
        + [pltpu.SemaphoreType.DMA(shape) for shape in DMA_ARRAYS.values()],
        compiler_params=pltpu.CompilerParams(collective_id=0, has_side_effects=True, vmem_limit_bytes=VMEM_LIMIT),
        name="step",
    )(x, cot, *weights, *vectors)


def tidy_kernel(frames, small, own, far, attn_in, act, grad_in, *rest):
    rows_out, outs, (attn, packed, packed_out, load_sem, store_sem) = rest[:9], rest[9:13], rest[13:]
    t = lax.axis_index("tensor")
    loads = [pltpu.make_async_copy(attn_in.at[level], attn.at[level], load_sem.at[level]) for level in range(LAYERS)]
    for copy in loads:
        copy.start()
    for n, out in ((0, act), (1, grad_in)):
        first = jnp.where(t == 0, own[n], far[n])[:frames]
        second = jnp.where(t == 0, far[n], own[n])[:frames]
        out[...] = jnp.stack([first, second], axis=1).astype(out.dtype)
    step = SMALL_ROWS // LAYERS
    for level in range(LAYERS):
        line = slice(level, level + 1)
        for n in range(ROW_UP):
            at = step * level + n
            rows_out[n][line, :] = small[0, at : at + 1, :]
        up = step * level + ROW_UP + t
        qkv = step * level + ROW_QKV + t
        for s in range(2):
            row = small[s, pl.ds(qkv, 1), :]
            rows_out[6][line, s * SUBH : (s + 1) * SUBH] = row[:, :SUBH]
            rows_out[7][line, s * SUBH : (s + 1) * SUBH] = row[:, 2 * SUBH : 3 * SUBH]
            rows_out[8][line, s * SUB : (s + 1) * SUB] = small[s, pl.ds(up, 1), :]
    stores = []
    for level in range(LAYERS):
        loads[level].wait()

        def body(rows):
            for n in range(3):
                parts = []
                for s in range(2):
                    block = [attn[level, s, g, rows, :] for g in range(3)]
                    pieces = (
                        [block[0][:, :SUBH]],
                        [block[0][:, SUBH:], block[1][:, :128]],
                        [block[1][:, 128:], block[2][:, :64]],
                    )
                    parts += pieces[n]
                packed[level, n, rows, :] = jnp.concatenate(parts, axis=1)

        rows_loop(D, 64, body)
        for s in range(2):
            packed_out[level, s * SUBH : (s + 1) * SUBH, :] = attn[level, s, 2][:, 64:].T
        for n in range(4):
            source = packed.at[level, n] if n < 3 else packed_out.at[level]
            stores.append(pltpu.make_async_copy(source, outs[n].at[level], store_sem.at[level, n]))
            stores[-1].start()
    for copy in stores:
        copy.wait()


def tidy(frames, small, pair_own, pair_far, attn):
    vmem = pl.BlockSpec(memory_space=pltpu.VMEM)
    anywhere = pl.BlockSpec(memory_space=pl.ANY)
    shapes = [((frames, 2, D), BF16), ((frames, 2, D), F32)]
    shapes += [((LAYERS, D), F32)] * 6 + [((LAYERS, 2 * SUBH), F32)] * 2 + [((LAYERS, 2 * SUB), F32)]
    wide = [((LAYERS, D, 2 * SUBH), F32)] * 3 + [((LAYERS, 2 * SUBH, D), F32)]
    act, grad_in, *rest = pl.pallas_call(
        functools.partial(tidy_kernel, frames),
        out_shape=[jax.ShapeDtypeStruct(*spec) for spec in shapes + wide],
        in_specs=[vmem] * 3 + [anywhere],
        out_specs=[vmem] * len(shapes) + [anywhere] * len(wide),
        scratch_shapes=[
            pltpu.VMEM((LAYERS, 2, 3, D, GW), F32),
            pltpu.VMEM((LAYERS, 3, D, 2 * SUBH), F32),
            pltpu.VMEM((LAYERS, 2 * SUBH, D), F32),
            pltpu.SemaphoreType.DMA((LAYERS,)),
            pltpu.SemaphoreType.DMA((LAYERS, 4)),
        ],
        compiler_params=pltpu.CompilerParams(vmem_limit_bytes=VMEM_LIMIT),
        name="tidy",
    )(small, pair_own, pair_far, attn)
    return [act.transpose(1, 0, 2), grad_in.transpose(1, 0, 2)] + rest


def local(
    inputs, cotangent, first_gain, first_shift, w_query, b_query, w_key, w_value, b_value, w_out, b_out,
    second_gain, second_shift, w_up, b_up, w_down, b_down,
):
    frames = inputs.shape[1]

    def padded(array):
        return jnp.pad(array.astype(F32), ((0, 0), (0, PAD - frames), (0, 0)))

    small, g_up, g_down, attn, pair_own, pair_far, *unused = step(
        frames, padded(inputs), padded(cotangent), (w_query, w_key, w_value, w_out, w_up, w_down),
        (first_gain, first_shift, second_gain, second_shift, b_out, b_down, b_query, b_value, b_up),
    )
    (
        act, grad_in, g_first_gain, g_first_shift, g_second_gain, g_second_shift, g_b_out, g_b_down, g_b_query, g_b_value, g_b_up,
        g_query, g_key, g_value, g_out,
    ) = tidy(frames, small, pair_own, pair_far, attn)
    return (
        act, grad_in, g_first_gain, g_first_shift, g_query, g_b_query, g_key, g_value, g_b_value, g_out, g_b_out,
        g_second_gain, g_second_shift, g_up, g_b_up, g_down, g_b_down,
    )


def solution(mesh):
    rows3 = P("dp", None, None)
    cols3 = P(None, None, "tensor")
    mid3 = P(None, "tensor", None)
    cols2 = P(None, "tensor")
    layout = (P(), P(), cols3, cols2, cols3, cols3, cols2, mid3, P(), P(), P(), cols3, cols2, mid3, P())
    return jax.shard_map(
        local,
        mesh=mesh,
        in_specs=(rows3, rows3) + layout,
        out_specs=(rows3, rows3) + layout,
        check_vma=False,
    )
```
